32 devices in a mesh: grp: 8 (over z, x), nar: 4 (over y, core).
Axes of the slice: x: 2, y: 2, z: 4, core: 2. Of those that a mesh axis runs over, the one named last changes fastest.
Arguments:
- run_desc: bfloat16 [131072, 256], P(('grp', 'nar')), may hold values from -48 to 48
- ref_desc: bfloat16 [4096, 256], P('nar'), may hold values from -6 to 6
- candidates: int32 [1024, 8], P(('grp', 'nar')), may hold values from 0 to 31, as said below
- live_slots: int32 [1024], P(('grp', 'nar')), may hold values from 1 to 8, as said below
- run_mass: float32 [131072], P(('grp', 'nar')), may hold values from 0.1 to 2
- ref_mass: float32 [4096], P('nar'), may hold values from 0.1 to 2
- ref_start: float32 [4096], P('nar'), may hold values from -62 to 42
Outputs:
- run_potential: float32 [131072], P(('grp', 'nar'))
- ref_potential: float32 [4096], P('nar')
The draws below stay inside these ranges and needn't reach their ends.
Inputs may be any that keep to these rules, and one draw needn't show every extreme that they name: `candidates`: each row holds 8 different reference block numbers; every reference block is the first entry of some row. `live_slots`: the first run block of each device has all 8 slots live.
All inputs are finite; a program needn't handle non-finite values.
Results may differ from the reference program's by a relative error of at most 0.0003.
Values may be sent and summed in bfloat16 or wider, within the bound.
No kernel may reach another device: no remote copies, remote signals or barrier semaphores. Data moves between devices by JAX's collectives and lax.ppermute only.
A program may use at most 128 MiB of HBM per device.

```python
import math
import jax
import jax.numpy as jnp
from jax import lax

D = 256
BLK = 128
TOPC = 8
ITERS = 3
RB_DEV = 32
RUNB = 1024
ROWS = 131072
REFB = 32
REF = 4096


def block_order(key):
    return jax.random.permutation(jax.random.fold_in(key, 301), REFB).astype(jnp.int32)


def candidate_table(key):
    key_scores = jax.random.fold_in(key, 302)
    run_index = jnp.arange(RUNB, dtype=jnp.int32)
    shuffled = block_order(key)
    leading = shuffled[run_index % REFB]
    rank_keys = jax.random.randint(key_scores, (RUNB, REFB - 1), 0, 1 << 20, dtype=jnp.int32)
    rank_keys = rank_keys * REFB + jnp.arange(REFB - 1, dtype=jnp.int32)[None, :]
    ordering = jnp.argsort(rank_keys, axis=1, stable=True).astype(jnp.int32)
    offsets = 1 + ordering[:, :TOPC - 1]
    trailing = (leading[:, None] + offsets) % REFB
    return jnp.concatenate([leading[:, None], trailing], axis=1).astype(jnp.int32)


def reference_base(key):
    drawn = jax.random.normal(jax.random.fold_in(key, 321), (REF, D), jnp.float32)
    drawn = jnp.clip(drawn, -6.0, 6.0)
    return drawn


def draw_candidates(key, part):
    return candidate_table(key)


def draw_live_slots(key, part):
    key_counts = jax.random.fold_in(key, 311)
    key_caps = jax.random.fold_in(key, 312)
    run_index = jnp.arange(RUNB, dtype=jnp.int32)
    drawn = jax.random.randint(key_counts, (RUNB,), 1, TOPC + 1, dtype=jnp.int32)
    device_cap = jax.random.randint(key_caps, (RUNB // RB_DEV,), 1, TOPC + 1, dtype=jnp.int32)
    capped = jnp.minimum(drawn, device_cap[run_index // RB_DEV])
    capped = jnp.where(run_index % RB_DEV == 0, TOPC, capped)
    capped = jnp.where(run_index == RB_DEV - 1, 1, capped)
    return capped.astype(jnp.int32)


def draw_ref_desc(key, part):
    return reference_base(key).astype(jnp.bfloat16)


def draw_run_desc(key, part):
    drawn = jax.random.normal(jax.random.fold_in(key, 331), (ROWS, D), jnp.float32)
    drawn = jnp.clip(drawn, -6.0, 6.0)
    ref_rows = reference_base(key)
    leading = candidate_table(key)[:, 0]
    chosen_blocks = (RUNB + 15) // 16
    picks = jnp.arange(3 * chosen_blocks, dtype=jnp.int32)
    run_rows = picks // 3 * 16 * BLK + picks % 3
    target = ref_rows[leading[picks // 3 * 16] * BLK]
    widen = 16.0 / math.sqrt(D)
    strength = widen * jnp.where(picks % 3 == 0, 3.2, 6.4)[:, None]
    extra = jnp.where(picks % 3 == 2, 0.6, 0.0)[:, None] * drawn[run_rows]
    drawn = drawn.at[run_rows].set(jnp.clip(strength * target + extra, -48.0, 48.0))
    return drawn.astype(jnp.bfloat16)


def draw_ref_start(key, part):
    cold_count = max(1, REFB // 16)
    shuffled = block_order(key)
    cold_block = jnp.zeros((REFB,), jnp.int32).at[shuffled[:cold_count]].set(1)
    hot_column = jax.random.randint(jax.random.fold_in(key, 344), (REFB,), 2, BLK, dtype=jnp.int32)
    cold_pick = jax.random.randint(jax.random.fold_in(key, 345), (REF,), 0, 8, dtype=jnp.int32)
    feature = jnp.arange(REF, dtype=jnp.int32)
    column = feature % BLK
    block = feature // BLK
    is_hot = column == hot_column[block]
    in_cold_block = cold_block[block] == 1
    cold_jitter = jnp.clip(jax.random.normal(jax.random.fold_in(key, 342), (REF,), jnp.float32), -3.0, 3.0)
    hot_jitter = jnp.clip(jax.random.normal(jax.random.fold_in(key, 346), (REF,), jnp.float32), -3.0, 3.0)
    drawn = jnp.clip(jax.random.normal(jax.random.fold_in(key, 341), (REF,), jnp.float32), -4.0, 4.0)
    is_cold = (cold_pick == 0) & jnp.logical_not(is_hot)
    cold_value = -60.0 + 0.5 * cold_jitter
    drawn = jnp.where(is_cold, cold_value, drawn)
    drawn = jnp.where(is_hot, 40.0 + 0.5 * hot_jitter, drawn)
    drawn = jnp.where(in_cold_block, cold_value, drawn)
    return drawn


def level_of(key, shape, cuts, least, high):
    loudness = 1.0
    for dim, blocks in cuts:
        draws = jax.random.uniform(jax.random.fold_in(jax.random.fold_in(key, 6), dim), (blocks,), jnp.float32, least / len(cuts), high / len(cuts))
        loudness = loudness * jnp.repeat(jnp.exp(draws), shape[dim] // blocks).reshape((-1,) + (1,) * (len(shape) - 1 - dim))
    return loudness


def setup_inputs(seed: int = 0) -> dict:
    seeds = jax.random.split(jax.random.key(seed), 8)
    return {
        "run_desc": draw_run_desc(jax.random.fold_in(seeds[7], 71), 0),
        "ref_desc": draw_ref_desc(jax.random.fold_in(seeds[7], 71), 0),
        "candidates": draw_candidates(jax.random.fold_in(seeds[7], 71), 0),
        "live_slots": draw_live_slots(jax.random.fold_in(seeds[7], 71), 0),
        "run_mass": jnp.clip(jnp.exp(math.log(2.0) - 2.9957323 * jax.random.uniform(seeds[4], (ROWS,), jnp.float32) ** level_of(seeds[4], (ROWS,), ((0, 32),), -0.2, 0.2)), 0.1, 2.0),
        "ref_mass": jnp.clip(jnp.exp(math.log(2.0) - 2.9957323 * jax.random.uniform(seeds[5], (REF,), jnp.float32) ** level_of(seeds[5], (REF,), ((0, 4),), -0.2, 0.2)), 0.1, 2.0),
        "ref_start": draw_ref_start(jax.random.fold_in(seeds[7], 71), 0),
    }


entropic = 0.5
floor_value = -1e+30

def tile_costs(run_desc, ref_desc, candidates):
    group_size = math.gcd(RUNB, 32)
    run_tiles = run_desc.reshape(RUNB // group_size, group_size, BLK, D)
    ref_tiles = ref_desc.reshape(REFB, BLK, D)
    picked_ids = candidates.reshape(RUNB // group_size, group_size, TOPC)

    def one_group(pieces):
        run_piece, id_piece = pieces
        picked = ref_tiles[id_piece].astype(jnp.float32)
        products = jnp.einsum('gid,gtjd->gtij', run_piece.astype(jnp.float32), picked)
        return -products / math.sqrt(D)
    tile_cost = lax.map(one_group, (run_tiles, picked_ids))
    return tile_cost.reshape(RUNB // group_size, group_size, TOPC, BLK, BLK)

def run_side(tile_cost, ref_potential, candidates, live_mask, run_mass):
    group_size = tile_cost.shape[1]
    picked = ref_potential.reshape(REFB, BLK)[candidates]
    picked = picked.reshape(RUNB // group_size, group_size, TOPC, BLK)
    masks = live_mask.reshape(RUNB // group_size, group_size, TOPC)

    def one_group(pieces):
        cost_piece, pick_piece, mask_piece = pieces
        scores = (pick_piece[:, :, None, :] - cost_piece) / entropic
        scores = jnp.where(mask_piece[:, :, None, None], scores, floor_value)
        row_peak = lax.optimization_barrier(jnp.max(scores, axis=(1, 3)))
        row_total = lax.optimization_barrier(jnp.sum(jnp.exp(scores - row_peak[:, None, :, None]), axis=(1, 3)))
        return (row_peak, row_total)
    row_peak, row_total = lax.map(one_group, (tile_cost, picked, masks))
    return entropic * jnp.log(run_mass) - entropic * (row_peak.reshape(-1) + jnp.log(row_total.reshape(-1)))

def ref_side(tile_cost, run_potential, candidates, live_mask, ref_mass):
    group_size = tile_cost.shape[1]
    runs_grouped = run_potential.reshape(RUNB // group_size, group_size, BLK)
    masks = live_mask.reshape(RUNB // group_size, group_size, TOPC)
    flat_ids = candidates.reshape(-1)

    def group_scores(cost_piece, run_piece, mask_piece):
        scores = (run_piece[:, None, :, None] - cost_piece) / entropic
        return jnp.where(mask_piece[:, :, None, None], scores, floor_value)

    def peaks_group(pieces):
        cost_piece, run_piece, mask_piece = pieces
        return lax.optimization_barrier(jnp.max(group_scores(cost_piece, run_piece, mask_piece), axis=2))
    col_peaks = lax.map(peaks_group, (tile_cost, runs_grouped, masks)).reshape(RUNB * TOPC, BLK)
    col_peak = jnp.full((REFB, BLK), floor_value, dtype=jnp.float32).at[flat_ids].max(col_peaks)
    peak_picked = col_peak[candidates].reshape(RUNB // group_size, group_size, TOPC, BLK)

    def totals_group(pieces):
        cost_piece, run_piece, mask_piece, peak_piece = pieces
        scores = group_scores(cost_piece, run_piece, mask_piece)
        return lax.optimization_barrier(jnp.sum(jnp.exp(scores - peak_piece[:, :, None, :]), axis=2))
    col_totals = lax.map(totals_group, (tile_cost, runs_grouped, masks, peak_picked)).reshape(RUNB * TOPC, BLK)
    col_total = jnp.zeros((REFB, BLK), dtype=jnp.float32).at[flat_ids].add(col_totals)
    log_mass = jnp.log(ref_mass).reshape(REFB, BLK)
    return (entropic * log_mass - entropic * (col_peak + jnp.log(col_total))).reshape(-1)

def reference(run_desc, ref_desc, candidates, live_slots, run_mass, ref_mass, ref_start):
    tile_cost = tile_costs(run_desc, ref_desc, candidates)
    live_mask = jnp.arange(TOPC, dtype=jnp.int32)[None, :] < live_slots[:, None]
    ref_potential = ref_start
    run_potential = jnp.zeros((ROWS,), dtype=jnp.float32)
    for iteration in range(ITERS):
        run_potential = run_side(tile_cost, ref_potential, candidates, live_mask, run_mass)
        ref_potential = ref_side(tile_cost, run_potential, candidates, live_mask, ref_mass)
    return (run_potential, ref_potential)
```

```python
import functools
import math

import jax
import jax.numpy as jnp
from jax import lax
from jax.experimental import pallas as pl
from jax.experimental.pallas import tpu as pltpu
from jax.sharding import PartitionSpec as P

BLK = 128
TOPC = 8
PAIRS = TOPC // 2
LOG2E = math.log2(math.e)
FLOOR = -1e30
VMEM_LIMIT = 56 * 1024 * 1024

vmem = pl.BlockSpec(memory_space=pltpu.VMEM)
smem = pl.BlockSpec(memory_space=pltpu.SMEM)


def group_size(run_blocks):
    for size in (4, 2):
        if run_blocks % size == 0:
            return size
    return 1


def by_groups(group_pairs, run_blocks, body):
    size = group_size(run_blocks)

    def step(group, carry):
        pairs = group_pairs[group]
        for count in range(1, PAIRS + 1):

            @pl.when(pairs == count)
            def _():
                body(count, [group * size + k for k in range(size)])

        return carry

    lax.fori_loop(0, run_blocks // size, step, 0)


def rows_of(block):
    return pl.ds(pl.multiple_of(block * BLK, BLK), BLK)


def pair_row(table, eff, place, pair):
    left = table[pl.ds(eff[place, 2 * pair], 1), :]
    right = table[pl.ds(eff[place, 2 * pair + 1], 1), :]
    return jnp.concatenate([left, right], axis=1)


def halves(join, tile):
    return join(tile[:, :BLK], tile[:, BLK:])


def first_kernel(group_pairs, order, cand, eff, run, ref, pot, log_mass, slot_ref, scores, lse, rows):
    run_blocks = order.shape[0]
    ref_blocks = lse.shape[0]
    scale = 2.0 * LOG2E / math.sqrt(run.shape[1])

    def body(pairs, places):
        for place in places:
            block = order[place]
            own = run[rows_of(block), :]
            peak = None
            for pair in range(pairs):
                both = jnp.concatenate(
                    [ref[rows_of(cand[place, 2 * pair + half]), :] for half in range(2)], axis=0
                )
                tile = lax.dot_general(
                    own, both, (((1,), (1,)), ((), ())), preferred_element_type=jnp.float32
                )
                tile = tile * scale
                scores[place, :, 2 * BLK * pair : 2 * BLK * (pair + 1)] = tile
                top = halves(jnp.maximum, tile + pair_row(pot, eff, place, pair))
                peak = top if peak is None else jnp.maximum(peak, top)
            peak = jnp.max(peak, axis=1, keepdims=True)
            total = None
            for pair in range(pairs):
                tile = scores[place, :, 2 * BLK * pair : 2 * BLK * (pair + 1)]
                part = halves(
                    jnp.add, jnp.exp2(tile + (pair_row(pot, eff, place, pair) - peak))
                )
                total = part if total is None else total + part
            total = jnp.sum(total, axis=1, keepdims=True)
            potential = log_mass[rows_of(block), :1] - (peak + jnp.log2(total))
            for pair in range(pairs):
                tile = scores[place, :, 2 * BLK * pair : 2 * BLK * (pair + 1)] + potential
                top = jnp.max(tile, axis=0, keepdims=True)
                row = top + jnp.log2(jnp.sum(jnp.exp2(tile - top), axis=0, keepdims=True))
                rows[pl.ds(place * TOPC + 2 * pair, 1), :] = row[:, :BLK]
                rows[pl.ds(place * TOPC + 2 * pair + 1, 1), :] = row[:, BLK:]

    by_groups(group_pairs, run_blocks, body)

    def join(block, carry):
        picked = jnp.where(slot_ref[...] == block, rows[...], FLOOR)
        top = jnp.max(picked, axis=0, keepdims=True)
        total = jnp.sum(jnp.exp2(picked - top), axis=0, keepdims=True)
        lse[pl.ds(block, 1), :] = top + jnp.log2(total)
        return carry

    lax.fori_loop(0, ref_blocks, join, 0)


def second_kernel(group_pairs, order, eff, scores, pot, log_mass, onehot, weights, peaks, sums, rows):
    run_blocks = order.shape[0]
    rows[...] = jnp.zeros_like(rows)

    def body(pairs, places):
        for place in places:
            block = order[place]
            peak = None
            for pair in range(pairs):
                tile = scores[place, :, 2 * BLK * pair : 2 * BLK * (pair + 1)]
                top = halves(jnp.maximum, tile + pair_row(pot, eff, place, pair))
                peak = top if peak is None else jnp.maximum(peak, top)
            peak = jnp.max(peak, axis=1, keepdims=True)
            peaks[rows_of(place), :] = jnp.broadcast_to(peak, (BLK, BLK))
            total = None
            for pair in range(pairs):
                tile = scores[place, :, 2 * BLK * pair : 2 * BLK * (pair + 1)]
                weight = jnp.exp2(tile + (pair_row(pot, eff, place, pair) - peak))
                weights[place, :, 2 * BLK * pair : 2 * BLK * (pair + 1)] = weight
                part = halves(jnp.add, weight)
                total = part if total is None else total + part
            total = jnp.sum(total, axis=1, keepdims=True)
            factor = jnp.exp2(log_mass[rows_of(block), :1] - jnp.log2(total))
            for pair in range(pairs):
                weight = weights[place, :, 2 * BLK * pair : 2 * BLK * (pair + 1)]
                row = jnp.sum(weight * factor, axis=0, keepdims=True)
                rows[pl.ds(place * TOPC + 2 * pair, 1), :] = row[:, :BLK]
                rows[pl.ds(place * TOPC + 2 * pair + 1, 1), :] = row[:, BLK:]

    by_groups(group_pairs, run_blocks, body)
    sums[...] = jnp.dot(
        onehot[...],
        rows[...],
        precision=lax.Precision.HIGHEST,
        preferred_element_type=jnp.float32,
    )


def third_kernel(group_pairs, order, eff, weights, peaks, gain, log_mass, onehot, out, sums, rows):
    run_blocks = order.shape[0]
    rows[...] = jnp.zeros_like(rows)
    diagonal = lax.broadcasted_iota(jnp.int32, (BLK, BLK), 0) == lax.broadcasted_iota(
        jnp.int32, (BLK, BLK), 1
    )

    def body(pairs, places):
        for place in places:
            block = order[place]
            total = None
            for pair in range(pairs):
                weight = weights[place, :, 2 * BLK * pair : 2 * BLK * (pair + 1)]
                part = halves(jnp.add, weight * pair_row(gain, eff, place, pair))
                total = part if total is None else total + part
            total = jnp.sum(total, axis=1, keepdims=True)
            log_factor = log_mass[rows_of(block), :1] - jnp.log2(total)
            factor = jnp.exp2(log_factor)
            potential = log_factor - peaks[rows_of(place), :1]
            out[pl.ds(block, 1), :] = jnp.sum(
                jnp.where(diagonal, potential * (0.5 / LOG2E), 0.0), axis=0, keepdims=True
            )
            for pair in range(pairs):
                weight = weights[place, :, 2 * BLK * pair : 2 * BLK * (pair + 1)]
                row = jnp.sum(weight * factor, axis=0, keepdims=True)
                rows[pl.ds(place * TOPC + 2 * pair, 1), :] = row[:, :BLK]
                rows[pl.ds(place * TOPC + 2 * pair + 1, 1), :] = row[:, BLK:]

    by_groups(group_pairs, run_blocks, body)
    sums[...] = jnp.dot(
        onehot[...],
        rows[...],
        precision=lax.Precision.HIGHEST,
        preferred_element_type=jnp.float32,
    )


def call(kernel, ins, outs, scratch):
    return pl.pallas_call(
        kernel,
        in_specs=ins,
        out_specs=[vmem] * len(outs),
        out_shape=outs,
        scratch_shapes=scratch,
        compiler_params=pltpu.CompilerParams(vmem_limit_bytes=VMEM_LIMIT),
    )


def log_sum(parts, axis):
    top = jnp.max(parts, axis=axis, keepdims=True)
    total = jnp.sum(jnp.exp2(parts - top), axis=axis, keepdims=True)
    return jnp.squeeze(top + jnp.log2(total), axis)


class Links:
    def __init__(self, groups, width):
        self.width = width
        self.devices = groups * width
        self.core = lax.axis_index("nar") % 2

    def swap(self, value, mask):
        pairs = [(k, k ^ mask) for k in range(self.devices)]
        return lax.ppermute(value, ("grp", "nar"), pairs)

    def half(self, value, which):
        count = value.shape[0] // 2
        return jnp.where(which == 0, value[:count], value[count:])

    def whole(self, value):
        other = self.swap(value, 1)
        low = jnp.where(self.core == 0, value, other)
        high = jnp.where(self.core == 0, other, value)
        return jnp.concatenate([low, high], axis=0)

    def reduce_half(self, value, join):
        kept = self.half(value, self.core)
        got = self.swap(self.half(value, 1 - self.core), 1)
        kept = join(jnp.stack([kept, got]), 0)
        chips = self.devices // 2
        sent = jnp.broadcast_to(kept[None], (chips,) + kept.shape)
        groups = [list(range(c, self.devices, 2)) for c in range(2)]
        parts = lax.all_to_all(
            sent, ("grp", "nar"), 0, 0, axis_index_groups=groups, tiled=True
        )
        return join(parts, 0)

    def reduce_own(self, value, join):
        own = value.shape[0] // self.width
        pieces = value.reshape(1, self.width, own, BLK)
        sent = jnp.broadcast_to(pieces, (self.devices // self.width,) + pieces.shape[1:])
        parts = lax.all_to_all(
            sent.reshape(self.devices, own, BLK), ("grp", "nar"), 0, 0, tiled=True
        )
        return join(parts, 0)

    def gather(self, value):
        held = {0: value}
        mask = self.width // 2
        while mask:
            held.update({key ^ mask: self.swap(part, mask) for key, part in list(held.items())})
            mask //= 2
        return [held[key] for key in range(self.width)]

    def arrange(self, parts):
        me = lax.axis_index("nar")
        bit = 1
        parts = list(parts)
        while bit < self.width:
            flip = (me & bit) != 0
            parts = [
                jnp.where(flip, parts[key ^ bit], parts[key]) for key in range(self.width)
            ]
            bit *= 2
        return jnp.concatenate(parts, axis=0)


def shards(run_desc, ref_desc, candidates, live_slots, run_mass, ref_mass, ref_start):
    run_blocks = candidates.shape[0]
    links = Links(lax.axis_size("grp"), lax.axis_size("nar"))
    own_blocks = ref_desc.shape[0] // BLK
    ref_blocks = own_blocks * links.width
    depth = run_desc.shape[1]
    f32 = jnp.float32

    small = jnp.concatenate(
        [
            (2.0 * LOG2E) * ref_start.reshape(1, own_blocks, BLK),
            jnp.log2(ref_mass).reshape(1, own_blocks, BLK),
        ]
    )
    small_all = links.gather(small)
    pot = links.arrange([part[0] for part in small_all])
    log_ref = links.arrange([part[1] for part in small_all])
    ref_all = links.arrange(links.gather(ref_desc))

    size = group_size(run_blocks)
    pairs = (live_slots + 1) // 2
    blocks = jnp.arange(run_blocks, dtype=jnp.int32)
    rank_key = pairs * run_blocks - blocks
    place = jnp.sum((rank_key[None, :] > rank_key[:, None]).astype(jnp.int32), axis=1)
    moved = place[None, :] == blocks[:, None]
    order = jnp.sum(jnp.where(moved, blocks[None, :], 0), axis=1)
    cand = jnp.sum(jnp.where(moved[:, :, None], candidates[None], 0), axis=1)
    live = jnp.sum(jnp.where(moved, live_slots[None, :], 0), axis=1)
    group_pairs = ((live + 1) // 2)[::size]
    slots = jnp.arange(TOPC, dtype=jnp.int32)
    eff = jnp.where(slots[None, :] < live[:, None], cand, ref_blocks)
    tiles = run_blocks * TOPC
    slot_ref = jnp.broadcast_to(eff.reshape(tiles, 1), (tiles, BLK))
    onehot = (
        eff.reshape(1, tiles) == jnp.arange(ref_blocks, dtype=jnp.int32)[:, None]
    ).astype(f32)
    log_mass = jnp.broadcast_to(
        jnp.log2(run_mass)[:, None], (run_blocks * BLK, BLK)
    )

    def padded(table):
        return jnp.concatenate([table, jnp.full((8, BLK), FLOOR, f32)], axis=0)

    rows = pltpu.VMEM((tiles, BLK), f32)
    score_shape = jax.ShapeDtypeStruct((run_blocks, BLK, TOPC * BLK), f32)
    table_shape = jax.ShapeDtypeStruct((ref_blocks, BLK), f32)
    rep_shape = jax.ShapeDtypeStruct((run_blocks * BLK, BLK), f32)
    scores, lse = call(
        first_kernel, [smem] * 4 + [vmem] * 5, [score_shape, table_shape], [rows]
    )(group_pairs, order, cand, eff, run_desc, ref_all, padded(pot), log_mass, slot_ref)

    log_half = links.half(log_ref, links.core)
    half = log_half - links.reduce_half(lse, log_sum)
    pot = links.whole(half)

    weights, peaks, sums = call(
        second_kernel, [smem] * 3 + [vmem] * 4, [score_shape, rep_shape, table_shape], [rows]
    )(group_pairs, order, eff, scores, padded(pot), log_mass, onehot)
    log_gain_half = log_half - jnp.log2(links.reduce_half(sums, jnp.sum))
    log_gain = links.whole(log_gain_half)
    pot = pot + log_gain
    gain = jnp.concatenate([jnp.exp2(log_gain), jnp.zeros((8, BLK), f32)], axis=0)

    run_pot, sums = call(
        third_kernel,
        [smem] * 3 + [vmem] * 5,
        [jax.ShapeDtypeStruct((run_blocks, BLK), f32), table_shape],
        [rows],
    )(group_pairs, order, eff, weights, peaks, gain, log_mass, onehot)
    total = links.reduce_own(sums, jnp.sum)
    start = lax.axis_index("nar") * own_blocks

    def mine(table):
        return lax.dynamic_slice_in_dim(table, start, own_blocks, 0)

    own = (mine(log_ref) + mine(pot) - mine(log_gain) - jnp.log2(total)) * (0.5 / LOG2E)
    return run_pot.reshape(-1), own.reshape(-1)


def solution(mesh):
    return jax.shard_map(
        shards,
        mesh=mesh,
        in_specs=(
            P(("grp", "nar"), None),
            P("nar", None),
            P(("grp", "nar"), None),
            P(("grp", "nar")),
            P(("grp", "nar")),
            P("nar"),
            P("nar"),
        ),
        out_specs=(P(("grp", "nar")), P("nar")),
        check_vma=False,
    )
```

```python
import functools
import math

import jax
import jax.numpy as jnp
from jax import lax
from jax.experimental import pallas as pl
from jax.experimental.pallas import tpu as pltpu
from jax.sharding import PartitionSpec as P

BLK = 128
TOPC = 8
PAIRS = TOPC // 2
LOG2E = math.log2(math.e)
FLOOR = -1e30
VMEM_LIMIT = 8 * 1024 * 1024

vmem = pl.BlockSpec(memory_space=pltpu.VMEM)
smem = pl.BlockSpec(memory_space=pltpu.SMEM)


def group_size(run_blocks):
    for size in (4, 2):
        if run_blocks % size == 0:
            return size
    return 1


def by_groups(group_pairs, run_blocks, body):
    size = group_size(run_blocks)

    def step(group, carry):
        pairs = group_pairs[group]
        for count in range(1, PAIRS + 1):

            @pl.when(pairs == count)
            def _():
                body(count, [group * size + k for k in range(size)])

        return carry

    lax.fori_loop(0, run_blocks // size, step, 0)


def rows_of(block):
    return pl.ds(pl.multiple_of(block * BLK, BLK), BLK)


def pair_row(table, eff, place, pair):
    left = table[pl.ds(eff[place, 2 * pair], 1), :]
    right = table[pl.ds(eff[place, 2 * pair + 1], 1), :]
    return jnp.concatenate([left, right], axis=1)


def halves(join, tile):
    return join(tile[:, :BLK], tile[:, BLK:])


def first_kernel(group_pairs, order, cand, eff, run, ref, pot, log_mass, slot_ref, scores, lse, rows):
    run_blocks = order.shape[0]
    ref_blocks = lse.shape[0]
    scale = 2.0 * LOG2E / math.sqrt(run.shape[1])

    def body(pairs, places):
        for place in places:
            block = order[place]
            own = run[rows_of(block), :]
            peak = None
            for pair in range(pairs):
                both = jnp.concatenate(
                    [ref[rows_of(cand[place, 2 * pair + half]), :] for half in range(2)], axis=0
                )
                tile = lax.dot_general(
                    own, both, (((1,), (1,)), ((), ())), preferred_element_type=jnp.float32
                )
                tile = tile * scale
                scores[place, :, 2 * BLK * pair : 2 * BLK * (pair + 1)] = tile
                top = halves(jnp.maximum, tile + pair_row(pot, eff, place, pair))
                peak = top if peak is None else jnp.maximum(peak, top)
            peak = jnp.max(peak, axis=1, keepdims=True)
            total = None
            for pair in range(pairs):
                tile = scores[place, :, 2 * BLK * pair : 2 * BLK * (pair + 1)]
                part = halves(
                    jnp.add, jnp.exp2(tile + (pair_row(pot, eff, place, pair) - peak))
                )
                total = part if total is None else total + part
            total = jnp.sum(total, axis=1, keepdims=True)
            potential = log_mass[rows_of(block), :1] - (peak + jnp.log2(total))
            for pair in range(pairs):
                tile = scores[place, :, 2 * BLK * pair : 2 * BLK * (pair + 1)] + potential
                top = jnp.max(tile, axis=0, keepdims=True)
                row = top + jnp.log2(jnp.sum(jnp.exp2(tile - top), axis=0, keepdims=True))
                rows[pl.ds(place * TOPC + 2 * pair, 1), :] = row[:, :BLK]
                rows[pl.ds(place * TOPC + 2 * pair + 1, 1), :] = row[:, BLK:]

    by_groups(group_pairs, run_blocks, body)

    def join(block, carry):
        picked = jnp.where(slot_ref[...] == block, rows[...], FLOOR)
        top = jnp.max(picked, axis=0, keepdims=True)
        total = jnp.sum(jnp.exp2(picked - top), axis=0, keepdims=True)
        lse[pl.ds(block, 1), :] = top + jnp.log2(total)
        return carry

    lax.fori_loop(0, ref_blocks, join, 0)


def second_kernel(group_pairs, order, eff, scores, pot, log_mass, onehot, weights, peaks, sums, rows):
    run_blocks = order.shape[0]
    rows[...] = jnp.zeros_like(rows)

    def body(pairs, places):
        for place in places:
            block = order[place]
            peak = None
            for pair in range(pairs):
                tile = scores[place, :, 2 * BLK * pair : 2 * BLK * (pair + 1)]
                top = halves(jnp.maximum, tile + pair_row(pot, eff, place, pair))
                peak = top if peak is None else jnp.maximum(peak, top)
            peak = jnp.max(peak, axis=1, keepdims=True)
            peaks[rows_of(place), :] = jnp.broadcast_to(peak, (BLK, BLK))
            total = None
            for pair in range(pairs):
                tile = scores[place, :, 2 * BLK * pair : 2 * BLK * (pair + 1)]
                weight = jnp.exp2(tile + (pair_row(pot, eff, place, pair) - peak))
                weights[place, :, 2 * BLK * pair : 2 * BLK * (pair + 1)] = weight
                part = halves(jnp.add, weight)
                total = part if total is None else total + part
            total = jnp.sum(total, axis=1, keepdims=True)
            factor = jnp.exp2(log_mass[rows_of(block), :1] - jnp.log2(total))
            for pair in range(pairs):
                weight = weights[place, :, 2 * BLK * pair : 2 * BLK * (pair + 1)]
                row = jnp.sum(weight * factor, axis=0, keepdims=True)
                rows[pl.ds(place * TOPC + 2 * pair, 1), :] = row[:, :BLK]
                rows[pl.ds(place * TOPC + 2 * pair + 1, 1), :] = row[:, BLK:]

    by_groups(group_pairs, run_blocks, body)
    sums[...] = jnp.dot(
        onehot[...],
        rows[...],
        precision=lax.Precision.HIGHEST,
        preferred_element_type=jnp.float32,
    )


def third_kernel(group_pairs, order, eff, weights, peaks, gain, log_mass, onehot, out, sums, rows):
    run_blocks = order.shape[0]
    rows[...] = jnp.zeros_like(rows)
    diagonal = lax.broadcasted_iota(jnp.int32, (BLK, BLK), 0) == lax.broadcasted_iota(
        jnp.int32, (BLK, BLK), 1
    )

    def body(pairs, places):
        for place in places:
            block = order[place]
            total = None
            for pair in range(pairs):
                weight = weights[place, :, 2 * BLK * pair : 2 * BLK * (pair + 1)]
                part = halves(jnp.add, weight * pair_row(gain, eff, place, pair))
                total = part if total is None else total + part
            total = jnp.sum(total, axis=1, keepdims=True)
            log_factor = log_mass[rows_of(block), :1] - jnp.log2(total)
            factor = jnp.exp2(log_factor)
            potential = log_factor - peaks[rows_of(place), :1]
            out[pl.ds(block, 1), :] = jnp.sum(
                jnp.where(diagonal, potential * (0.5 / LOG2E), 0.0), axis=0, keepdims=True
            )
            for pair in range(pairs):
                weight = weights[place, :, 2 * BLK * pair : 2 * BLK * (pair + 1)]
                row = jnp.sum(weight * factor, axis=0, keepdims=True)
                rows[pl.ds(place * TOPC + 2 * pair, 1), :] = row[:, :BLK]
                rows[pl.ds(place * TOPC + 2 * pair + 1, 1), :] = row[:, BLK:]

    by_groups(group_pairs, run_blocks, body)
    sums[...] = jnp.dot(
        onehot[...],
        rows[...],
        precision=lax.Precision.HIGHEST,
        preferred_element_type=jnp.float32,
    )


def call(kernel, ins, outs, scratch, aliases={}):
    return pl.pallas_call(
        kernel,
        in_specs=ins,
        out_specs=[vmem] * len(outs),
        out_shape=outs,
        scratch_shapes=scratch,
        input_output_aliases=aliases,
        compiler_params=pltpu.CompilerParams(vmem_limit_bytes=VMEM_LIMIT),
    )


def by_twos(join, parts):
    while len(parts) > 1:
        parts = [join(*parts[k : k + 2]) for k in range(0, len(parts), 2)]
    return parts[0]


def log_sum(parts):
    top = by_twos(jnp.maximum, parts)
    return top + jnp.log2(by_twos(jnp.add, [jnp.exp2(part - top) for part in parts]))


def plain_sum(parts):
    return by_twos(jnp.add, parts)


class Links:
    def __init__(self, groups, width):
        self.width = width
        self.devices = groups * width

    def swap(self, value, mask):
        pairs = [(k, k ^ mask) for k in range(self.devices)]
        return lax.ppermute(value, ("grp", "nar"), pairs)

    def reduce_all(self, value, join):
        masks, bit = [[1]], 2
        while bit < self.devices:
            wide = 4 * bit <= self.devices
            masks.append([bit, 2 * bit, 3 * bit] if wide else [bit])
            bit *= 4 if wide else 2
        for stage in masks:
            value = join([value] + [self.swap(value, mask) for mask in stage])
        return value

    def reduce_own(self, value, join):
        own = value.shape[0] // self.width
        pieces = value.reshape(1, self.width, own, BLK)
        sent = jnp.broadcast_to(pieces, (self.devices // self.width,) + pieces.shape[1:])
        parts = lax.all_to_all(
            sent.reshape(self.devices, own, BLK), ("grp", "nar"), 0, 0, tiled=True
        )
        return join(list(parts))

    def gather(self, value):
        held = {0: value}
        mask = self.width // 2
        while mask:
            held.update({key ^ mask: self.swap(part, mask) for key, part in list(held.items())})
            mask //= 2
        return [held[key] for key in range(self.width)]

    def arrange(self, parts):
        me = lax.axis_index("nar")
        bit = 1
        parts = list(parts)
        while bit < self.width:
            flip = (me & bit) != 0
            parts = [
                jnp.where(flip, parts[key ^ bit], parts[key]) for key in range(self.width)
            ]
            bit *= 2
        return jnp.concatenate(parts, axis=0)


def shards(run_desc, ref_desc, candidates, live_slots, run_mass, ref_mass, ref_start):
    run_blocks = candidates.shape[0]
    links = Links(lax.axis_size("grp"), lax.axis_size("nar"))
    own_blocks = ref_desc.shape[0] // BLK
    ref_blocks = own_blocks * links.width
    depth = run_desc.shape[1]
    f32 = jnp.float32

    small = jnp.concatenate(
        [
            (2.0 * LOG2E) * ref_start.reshape(1, own_blocks, BLK),
            jnp.log2(ref_mass).reshape(1, own_blocks, BLK),
        ]
    )
    small_all = links.gather(small)
    pot = links.arrange([part[0] for part in small_all])
    log_ref = links.arrange([part[1] for part in small_all])
    ref_all = links.arrange(links.gather(ref_desc))

    size = group_size(run_blocks)
    pairs = (live_slots + 1) // 2
    blocks = jnp.arange(run_blocks, dtype=jnp.int32)
    rank_key = pairs * run_blocks - blocks
    place = jnp.sum((rank_key[None, :] > rank_key[:, None]).astype(jnp.int32), axis=1)
    moved = place[None, :] == blocks[:, None]
    order = jnp.sum(jnp.where(moved, blocks[None, :], 0), axis=1)
    cand = jnp.sum(jnp.where(moved[:, :, None], candidates[None], 0), axis=1)
    live = jnp.sum(jnp.where(moved, live_slots[None, :], 0), axis=1)
    group_pairs = ((live + 1) // 2)[::size]
    slots = jnp.arange(TOPC, dtype=jnp.int32)
    eff = jnp.where(slots[None, :] < live[:, None], cand, ref_blocks)
    tiles = run_blocks * TOPC
    slot_ref = jnp.broadcast_to(eff.reshape(tiles, 1), (tiles, BLK))
    onehot = (
        eff.reshape(1, tiles) == jnp.arange(ref_blocks, dtype=jnp.int32)[:, None]
    ).astype(f32)
    log_mass = jnp.broadcast_to(
        jnp.log2(run_mass)[:, None], (run_blocks * BLK, BLK)
    )

    def padded(table):
        return jnp.concatenate([table, jnp.full((8, BLK), FLOOR, f32)], axis=0)

    rows = pltpu.VMEM((tiles, BLK), f32)
    score_shape = pltpu.VMEM((run_blocks, BLK, TOPC * BLK), f32)
    table_shape = jax.ShapeDtypeStruct((ref_blocks, BLK), f32)
    rep_shape = pltpu.VMEM((run_blocks * BLK, BLK), f32)
    scores, lse = call(
        first_kernel, [smem] * 4 + [vmem] * 5, [score_shape, table_shape], [rows]
    )(group_pairs, order, cand, eff, run_desc, ref_all, padded(pot), log_mass, slot_ref)

    pot = log_ref - links.reduce_all(lse, log_sum)

    weights, peaks, sums = call(
        second_kernel, [smem] * 3 + [vmem] * 4, [score_shape, rep_shape, table_shape], [rows], {3: 0}
    )(group_pairs, order, eff, pltpu.with_memory_space_constraint(scores, pltpu.VMEM), padded(pot), log_mass, onehot)
    log_gain = log_ref - jnp.log2(links.reduce_all(sums, plain_sum))
    pot = pot + log_gain
    gain = jnp.concatenate([jnp.exp2(log_gain), jnp.zeros((8, BLK), f32)], axis=0)

    run_pot, sums = call(
        third_kernel,
        [smem] * 3 + [vmem] * 5,
        [jax.ShapeDtypeStruct((run_blocks, BLK), f32), table_shape],
        [rows],
    )(group_pairs, order, eff, pltpu.with_memory_space_constraint(weights, pltpu.VMEM), pltpu.with_memory_space_constraint(peaks, pltpu.VMEM), gain, log_mass, onehot)
    total = links.reduce_own(sums, plain_sum)
    start = lax.axis_index("nar") * own_blocks

    def mine(table):
        return lax.dynamic_slice_in_dim(table, start, own_blocks, 0)

    own = (mine(log_ref) + mine(pot) - mine(log_gain) - jnp.log2(total)) * (0.5 / LOG2E)
    return run_pot.reshape(-1), own.reshape(-1)


def solution(mesh):
    return jax.shard_map(
        shards,
        mesh=mesh,
        in_specs=(
            P(("grp", "nar"), None),
            P("nar", None),
            P(("grp", "nar"), None),
            P(("grp", "nar")),
            P(("grp", "nar")),
            P("nar"),
            P("nar"),
        ),
        out_specs=(P(("grp", "nar")), P("nar")),
        check_vma=False,
    )
```

```python
import functools
import math

import jax
import jax.numpy as jnp
from jax import lax
from jax.experimental import pallas as pl
from jax.experimental.pallas import tpu as pltpu
from jax.sharding import PartitionSpec as P

BLK = 128
TOPC = 8
JOINED = 8
LOG2E = math.log2(math.e)
FLOOR = -1e30
VMEM_LIMIT = 8 * 1024 * 1024

vmem = pl.BlockSpec(memory_space=pltpu.VMEM)
smem = pl.BlockSpec(memory_space=pltpu.SMEM)


def group_size(run_blocks):
    for size in (4, 2):
        if run_blocks % size == 0:
            return size
    return 1


class Table:
    def __init__(self, ref, run_blocks):
        self.ref = ref
        self.run_blocks = run_blocks

    def order(self, place):
        return self.ref[place]

    def live(self, place):
        return self.ref[self.run_blocks + place]

    def cand(self, place, slot):
        return self.ref[2 * self.run_blocks + place * TOPC + slot]

    def eff(self, place, slot):
        return self.ref[(2 + TOPC) * self.run_blocks + place * TOPC + slot]

    def offset(self, index):
        return self.ref[(2 + 2 * TOPC) * self.run_blocks + index]

    def by_groups(self, body, grain):
        size = group_size(self.run_blocks)

        def step(group, carry):
            most = self.live(group * size)
            for count in range(grain, TOPC + 1, grain):

                @pl.when((most <= count) & (most > count - grain))
                def _():
                    body(count, [group * size + k for k in range(size)])

            return carry

        lax.fori_loop(0, self.run_blocks // size, step, 0)


def rows_of(block):
    return pl.ds(pl.multiple_of(block * BLK, BLK), BLK)


def side(parts):
    return parts[0] if len(parts) == 1 else jnp.concatenate(parts, axis=1)


def pair_row(values, table, place, pair):
    return side([values[pl.ds(table.eff(place, slot), 1), :] for slot in pair])


def spread(column):
    return jnp.broadcast_to(column, (BLK, BLK))


def wide(tile, pair):
    return side([tile] * len(pair))


def pairs_of(count):
    return [range(first, min(first + 2, count)) for first in range(0, count, 2)]


def span(pair):
    return slice(BLK * pair[0], BLK * (pair[-1] + 1))


def put_rows(rows, place, pair, row):
    for index, slot in enumerate(pair):
        rows[pl.ds(place * TOPC + slot, 1), :] = row[:, BLK * index : BLK * (index + 1)]


def halves(join, tile):
    return tile if tile.shape[1] == BLK else join(tile[:, :BLK], tile[:, BLK:])


def first_kernel(table, run_hbm, mass_hbm, own_hbm, pot, slot_ref, *rest):
    pieces, (scores, log_mass, lse, rows, ref, run, run_mass, own, arrived) = rest[:-9], rest[-9:]
    run_blocks = scores.shape[0]
    table = Table(table, run_blocks)
    copies = [
        pltpu.make_async_copy(mass_hbm, run_mass, arrived.at[0]),
        pltpu.make_async_copy(own_hbm, own, arrived.at[1]),
        pltpu.make_async_copy(run_hbm, run, arrived.at[2]),
    ]
    for copy in copies:
        copy.start()
    own_blocks = own_hbm.shape[0] // BLK
    for index, piece in enumerate(pieces):
        start = table.offset(index + 1) // BLK
        for block in range(own_blocks):
            ref[start + block] = piece[BLK * block : BLK * (block + 1), :].T
    copies[0].wait()

    def fill(block, carry):
        row = jnp.log2(run_mass[pl.ds(block, 1), :])
        log_mass[rows_of(block), :] = jnp.broadcast_to(row, (BLK, BLK)).T
        return carry

    lax.fori_loop(0, run_blocks, fill, 0, unroll=math.gcd(run_blocks, 8))
    copies[1].wait()
    for block in range(own_blocks):
        ref[table.offset(0) // BLK + block] = own[BLK * block : BLK * (block + 1), :].T
    copies[2].wait()
    ref_blocks = lse.shape[0]
    scale = 2.0 * LOG2E / math.sqrt(run.shape[1])

    def body(count, places):
        peaks = []
        for place in places:
            mine = run[rows_of(table.order(place)), :]
            peak = None
            for pair in pairs_of(count):
                both = jnp.concatenate(
                    [ref[table.cand(place, slot)] for slot in pair], axis=1
                )
                tile = lax.dot_general(
                    mine, both, (((1,), (0,)), ((), ())), preferred_element_type=jnp.float32
                )
                tile = tile * scale
                scores[place, :, span(pair)] = tile
                top = halves(jnp.maximum, tile + pair_row(pot, table, place, pair))
                peak = top if peak is None else jnp.maximum(peak, top)
            peaks.append(peak)
        peaks = [spread(jnp.max(peak, axis=1, keepdims=True)) for peak in peaks]
        totals = []
        for place, peak in zip(places, peaks):
            total = None
            for pair in pairs_of(count):
                tile = scores[place, :, span(pair)] + pair_row(pot, table, place, pair)
                part = halves(jnp.add, jnp.exp2(tile - wide(peak, pair)))
                total = part if total is None else total + part
            totals.append(total)
        totals = [spread(jnp.sum(total, axis=1, keepdims=True)) for total in totals]
        potentials = [
            log_mass[rows_of(table.order(place)), :] - (peak + jnp.log2(total))
            for place, peak, total in zip(places, peaks, totals)
        ]
        for place, potential in zip(places, potentials):
            for pair in pairs_of(count):
                tile = scores[place, :, span(pair)] + wide(potential, pair)
                top = jnp.max(tile, axis=0, keepdims=True)
                row = top + jnp.log2(jnp.sum(jnp.exp2(tile - top), axis=0, keepdims=True))
                put_rows(rows, place, pair, row)

    table.by_groups(body, 1)

    def join(step, carry):
        for k in range(JOINED):
            block = step * JOINED + k
            picked = jnp.where(slot_ref[...] == block, rows[...], FLOOR)
            top = jnp.max(picked, axis=0, keepdims=True)
            total = jnp.sum(jnp.exp2(picked - top), axis=0, keepdims=True)
            lse[pl.ds(block, 1), :] = top + jnp.log2(total)
        return carry

    lax.fori_loop(0, ref_blocks // JOINED, join, 0)


def second_kernel(table, scores, pot, log_mass, onehot, weights, peaks, sums, rows):
    run_blocks = weights.shape[0]
    table = Table(table, run_blocks)
    rows[...] = jnp.zeros_like(rows)

    def body(count, places):
        tops = []
        for place in places:
            peak = None
            for pair in pairs_of(count):
                tile = scores[place, :, span(pair)] + pair_row(pot, table, place, pair)
                top = halves(jnp.maximum, tile)
                peak = top if peak is None else jnp.maximum(peak, top)
            tops.append(peak)
        tops = [spread(jnp.max(peak, axis=1, keepdims=True)) for peak in tops]
        totals = []
        for place, peak in zip(places, tops):
            peaks[rows_of(place), :] = peak
            total = None
            for pair in pairs_of(count):
                tile = scores[place, :, span(pair)] + pair_row(pot, table, place, pair)
                weight = jnp.exp2(tile - wide(peak, pair))
                weights[place, :, span(pair)] = weight
                part = halves(jnp.add, weight)
                total = part if total is None else total + part
            totals.append(total)
        totals = [spread(jnp.sum(total, axis=1, keepdims=True)) for total in totals]
        factors = [
            jnp.exp2(log_mass[rows_of(table.order(place)), :] - jnp.log2(total))
            for place, total in zip(places, totals)
        ]
        for place, factor in zip(places, factors):
            for pair in pairs_of(count):
                weight = weights[place, :, span(pair)] * wide(factor, pair)
                put_rows(rows, place, pair, jnp.sum(weight, axis=0, keepdims=True))

    table.by_groups(body, 2)
    sums[...] = jnp.dot(
        onehot[...],
        rows[...],
        precision=lax.Precision.HIGHEST,
        preferred_element_type=jnp.float32,
    )


def third_kernel(table, weights, peaks, gain, log_mass, onehot, out, sums, rows):
    run_blocks = weights.shape[0]
    table = Table(table, run_blocks)
    rows[...] = jnp.zeros_like(rows)
    diagonal = lax.broadcasted_iota(jnp.int32, (BLK, BLK), 0) == lax.broadcasted_iota(
        jnp.int32, (BLK, BLK), 1
    )

    def body(count, places):
        totals = []
        for place in places:
            total = None
            for pair in pairs_of(count):
                weight = weights[place, :, span(pair)] * pair_row(gain, table, place, pair)
                part = halves(jnp.add, weight)
                total = part if total is None else total + part
            totals.append(total)
        totals = [spread(jnp.sum(total, axis=1, keepdims=True)) for total in totals]
        factors = []
        for place, total in zip(places, totals):
            block = table.order(place)
            log_factor = log_mass[rows_of(block), :] - jnp.log2(total)
            factors.append(jnp.exp2(log_factor))
            potential = (log_factor - peaks[rows_of(place), :]) * (0.5 / LOG2E)
            out[pl.ds(block, 1), :] = jnp.sum(
                jnp.where(diagonal, potential, 0.0), axis=0, keepdims=True
            )
        for place, factor in zip(places, factors):
            for pair in pairs_of(count):
                weight = weights[place, :, span(pair)] * wide(factor, pair)
                put_rows(rows, place, pair, jnp.sum(weight, axis=0, keepdims=True))

    table.by_groups(body, 2)
    total = jnp.dot(
        onehot[...],
        rows[...],
        precision=lax.Precision.HIGHEST,
        preferred_element_type=jnp.float32,
    )
    for group in range(sums.shape[0]):
        sums[group] = total


def call(kernel, ins, outs, scratch, aliases={}):
    return pl.pallas_call(
        kernel,
        in_specs=ins,
        out_specs=[vmem] * len(outs),
        out_shape=outs,
        scratch_shapes=scratch,
        input_output_aliases=aliases,
        compiler_params=pltpu.CompilerParams(vmem_limit_bytes=VMEM_LIMIT),
    )


def by_twos(join, parts):
    while len(parts) > 1:
        parts = [join(*parts[k : k + 2]) for k in range(0, len(parts), 2)]
    return parts[0]


def log_sum(parts):
    top = by_twos(jnp.maximum, parts)
    return top + jnp.log2(by_twos(jnp.add, [jnp.exp2(part - top) for part in parts]))


def plain_sum(parts):
    return by_twos(jnp.add, parts)


class Links:
    def __init__(self, groups, width):
        self.width = width
        self.groups = groups
        self.devices = groups * width

    def swap(self, value, mask):
        pairs = [(k, k ^ mask) for k in range(self.devices)]
        return lax.ppermute(value, ("grp", "nar"), pairs)

    def reduce_all(self, value, join):
        masks, bit = [[1]], 2
        while bit < self.devices:
            wide = 4 * bit <= self.devices
            masks.append([bit, 2 * bit, 3 * bit] if wide else [bit])
            bit *= 4 if wide else 2
        for stage in masks:
            value = join([value] + [self.swap(value, mask) for mask in stage])
        return value

    def reduce_own(self, copies, join):
        own = copies.shape[1] // self.width
        sent = copies.reshape(self.devices, own, BLK)
        return join(list(lax.all_to_all(sent, ("grp", "nar"), 0, 0, tiled=True)))

    def gather(self, value):
        held = {0: value}
        mask = self.width // 2
        while mask:
            held.update({key ^ mask: self.swap(part, mask) for key, part in list(held.items())})
            mask //= 2
        return [held[key] for key in range(self.width)]

    def offsets(self, rows):
        me = lax.axis_index("nar")
        return jnp.stack([(key ^ me) * rows for key in range(self.width)]).astype(jnp.int32)

    def arrange(self, parts):
        me = lax.axis_index("nar")
        bit = 1
        parts = list(parts)
        while bit < self.width:
            flip = (me & bit) != 0
            parts = [
                jnp.where(flip, parts[key ^ bit], parts[key]) for key in range(self.width)
            ]
            bit *= 2
        return jnp.concatenate(parts, axis=0)


def shards(run_desc, ref_desc, candidates, live_slots, run_mass, ref_mass, ref_start):
    run_blocks = candidates.shape[0]
    links = Links(lax.axis_size("grp"), lax.axis_size("nar"))
    own_blocks = ref_desc.shape[0] // BLK
    ref_blocks = own_blocks * links.width
    depth = run_desc.shape[1]
    f32 = jnp.float32

    shape = (own_blocks, BLK)
    pot = links.arrange(links.gather(ref_start.reshape(shape))) * (2.0 * LOG2E)
    log_ref = jnp.log2(links.arrange(links.gather(ref_mass.reshape(shape))))
    pieces = links.gather(ref_desc)
    offsets = links.offsets(ref_desc.shape[0])
    blocks = jnp.arange(run_blocks, dtype=jnp.int32)
    rank_key = live_slots * run_blocks - blocks
    place = jnp.sum((rank_key[None, :] > rank_key[:, None]).astype(jnp.int32), axis=1)
    moved = place[None, :] == blocks[:, None]
    order = jnp.sum(jnp.where(moved, blocks[None, :], 0), axis=1)
    cand = jnp.sum(jnp.where(moved[:, :, None], candidates[None], 0), axis=1)
    live = jnp.sum(jnp.where(moved, live_slots[None, :], 0), axis=1)
    slots = jnp.arange(TOPC, dtype=jnp.int32)
    eff = jnp.where(slots[None, :] < live[:, None], cand, ref_blocks)
    table = jnp.concatenate([order, live, cand.reshape(-1), eff.reshape(-1), offsets])
    tiles = run_blocks * TOPC
    slot_ref = jnp.broadcast_to(eff.reshape(tiles, 1), (tiles, BLK))
    onehot = (
        eff.reshape(1, tiles) == jnp.arange(ref_blocks, dtype=jnp.int32)[:, None]
    ).astype(f32)
    def padded(table):
        return jnp.concatenate([table, jnp.full((8, BLK), FLOOR, f32)], axis=0)

    rows = pltpu.VMEM((tiles, BLK), f32)
    score_shape = pltpu.VMEM((run_blocks, BLK, TOPC * BLK), f32)
    table_shape = jax.ShapeDtypeStruct((ref_blocks, BLK), f32)
    rep_shape = pltpu.VMEM((run_blocks * BLK, BLK), f32)
    scores, log_mass, lse = call(
        first_kernel,
        [smem] + [pl.BlockSpec(memory_space=pltpu.HBM)] * 3 + [vmem] * (2 + len(pieces) - 1),
        [score_shape, rep_shape, table_shape],
        [
            rows,
            pltpu.VMEM((ref_blocks, depth, BLK), ref_desc.dtype),
            pltpu.VMEM(run_desc.shape, run_desc.dtype),
            pltpu.VMEM((run_blocks, BLK), f32),
            pltpu.VMEM(ref_desc.shape, ref_desc.dtype),
            pltpu.SemaphoreType.DMA((3,)),
        ],
    )(
        table,
        pltpu.with_memory_space_constraint(run_desc, pltpu.HBM),
        pltpu.with_memory_space_constraint(run_mass.reshape(run_blocks, BLK), pltpu.HBM),
        pltpu.with_memory_space_constraint(pieces[0], pltpu.HBM),
        padded(pot),
        slot_ref,
        *pieces[1:],
    )

    pot = log_ref - links.reduce_all(lse, log_sum)

    weights, peaks, sums = call(
        second_kernel, [smem] + [vmem] * 4, [score_shape, rep_shape, table_shape], [rows], {1: 0}
    )(table, pltpu.with_memory_space_constraint(scores, pltpu.VMEM), padded(pot), log_mass, onehot)
    log_gain = log_ref - jnp.log2(links.reduce_all(sums, plain_sum))
    pot = pot + log_gain
    gain = jnp.concatenate([jnp.exp2(log_gain), jnp.zeros((8, BLK), f32)], axis=0)

    run_pot, sums = call(
        third_kernel,
        [smem] + [vmem] * 5,
        [
            jax.ShapeDtypeStruct((run_blocks, BLK), f32),
            jax.ShapeDtypeStruct((links.groups, ref_blocks, BLK), f32),
        ],
        [rows],
    )(table, pltpu.with_memory_space_constraint(weights, pltpu.VMEM), pltpu.with_memory_space_constraint(peaks, pltpu.VMEM), gain, log_mass, onehot)
    total = links.reduce_own(sums, plain_sum)
    start = lax.axis_index("nar") * own_blocks

    def mine(table):
        return lax.dynamic_slice_in_dim(table, start, own_blocks, 0)

    own = (mine(log_ref) + mine(pot) - mine(log_gain) - jnp.log2(total)) * (0.5 / LOG2E)
    return run_pot.reshape(-1), own.reshape(-1)


def solution(mesh):
    return jax.shard_map(
        shards,
        mesh=mesh,
        in_specs=(
            P(("grp", "nar"), None),
            P("nar", None),
            P(("grp", "nar"), None),
            P(("grp", "nar")),
            P(("grp", "nar")),
            P("nar"),
            P("nar"),
        ),
        out_specs=(P(("grp", "nar")), P("nar")),
        check_vma=False,
    )
```

```python
import functools
import math

import jax
import jax.numpy as jnp
from jax import lax
from jax.experimental import pallas as pl
from jax.experimental.pallas import tpu as pltpu
from jax.sharding import PartitionSpec as P

BLK = 128
TOPC = 8
JOINED = 8
LOG2E = math.log2(math.e)
FLOOR = -1e30
VMEM_LIMIT = 8 * 1024 * 1024

vmem = pl.BlockSpec(memory_space=pltpu.VMEM)
smem = pl.BlockSpec(memory_space=pltpu.SMEM)


def group_size(run_blocks):
    for size in (4, 2):
        if run_blocks % size == 0:
            return size
    return 1


class Table:
    def __init__(self, ref, run_blocks):
        self.ref = ref
        self.run_blocks = run_blocks

    def order(self, place):
        return self.ref[place]

    def live(self, place):
        return self.ref[self.run_blocks + place]

    def cand(self, place, slot):
        return self.ref[2 * self.run_blocks + place * TOPC + slot]

    def eff(self, place, slot):
        return self.ref[(2 + TOPC) * self.run_blocks + place * TOPC + slot]

    def offset(self, index):
        return self.ref[(2 + 2 * TOPC) * self.run_blocks + index]

    def by_groups(self, body, grain):
        size = group_size(self.run_blocks)

        def step(group, carry):
            most = self.live(group * size)
            for count in range(grain, TOPC + 1, grain):

                @pl.when((most <= count) & (most > count - grain))
                def _():
                    body(count, [group * size + k for k in range(size)])

            return carry

        lax.fori_loop(0, self.run_blocks // size, step, 0)


def rows_of(block):
    return pl.ds(pl.multiple_of(block * BLK, BLK), BLK)


def side(parts):
    return parts[0] if len(parts) == 1 else jnp.concatenate(parts, axis=1)


def pair_row(values, table, place, pair):
    return side([values[pl.ds(table.eff(place, slot), 1), :] for slot in pair])


def spread(column):
    return jnp.broadcast_to(column, (BLK, BLK))


def wide(tile, pair):
    return side([tile] * len(pair))


def pairs_of(count):
    return [range(first, min(first + 2, count)) for first in range(0, count, 2)]


def span(pair):
    return slice(BLK * pair[0], BLK * (pair[-1] + 1))


def put_rows(rows, place, pair, row):
    for index, slot in enumerate(pair):
        rows[pl.ds(place * TOPC + slot, 1), :] = row[:, BLK * index : BLK * (index + 1)]


def halves(join, tile):
    return tile if tile.shape[1] == BLK else join(tile[:, :BLK], tile[:, BLK:])


def first_kernel(table, run_hbm, mass_hbm, own_hbm, pot, slot_ref, *rest):
    pieces, (scores, log_mass, lse, rows, ref, run, run_mass, own, arrived) = rest[:-9], rest[-9:]
    run_blocks = scores.shape[0]
    table = Table(table, run_blocks)
    copies = [
        pltpu.make_async_copy(mass_hbm, run_mass, arrived.at[0]),
        pltpu.make_async_copy(own_hbm, own, arrived.at[1]),
        pltpu.make_async_copy(run_hbm, run, arrived.at[2]),
    ]
    for copy in copies:
        copy.start()
    own_blocks = own_hbm.shape[0] // BLK
    for index, piece in enumerate(pieces):
        start = table.offset(index + 1) // BLK
        for block in range(piece.shape[0] // BLK):
            ref[start + block] = piece[BLK * block : BLK * (block + 1), :].T
    copies[0].wait()

    def fill(block, carry):
        row = jnp.log2(run_mass[pl.ds(block, 1), :])
        log_mass[rows_of(block), :] = jnp.broadcast_to(row, (BLK, BLK)).T
        return carry

    lax.fori_loop(0, run_blocks, fill, 0, unroll=math.gcd(run_blocks, 8))
    copies[1].wait()
    for block in range(own_blocks):
        ref[table.offset(0) // BLK + block] = own[BLK * block : BLK * (block + 1), :].T
    copies[2].wait()
    ref_blocks = lse.shape[0]
    scale = 2.0 * LOG2E / math.sqrt(run.shape[1])

    def body(count, places):
        peaks = []
        for place in places:
            mine = run[rows_of(table.order(place)), :]
            peak = None
            for pair in pairs_of(count):
                both = jnp.concatenate(
                    [ref[table.cand(place, slot)] for slot in pair], axis=1
                )
                tile = lax.dot_general(
                    mine, both, (((1,), (0,)), ((), ())), preferred_element_type=jnp.float32
                )
                tile = tile * scale
                scores[place, :, span(pair)] = tile
                if len(pair) == 1:
                    scores[place, :, span([count])] = jnp.zeros_like(tile)
                top = halves(jnp.maximum, tile + pair_row(pot, table, place, pair))
                peak = top if peak is None else jnp.maximum(peak, top)
            peaks.append(peak)
        peaks = [spread(jnp.max(peak, axis=1, keepdims=True)) for peak in peaks]
        totals = []
        for place, peak in zip(places, peaks):
            total = None
            for pair in pairs_of(count):
                tile = scores[place, :, span(pair)] + pair_row(pot, table, place, pair)
                part = halves(jnp.add, jnp.exp2(tile - wide(peak, pair)))
                total = part if total is None else total + part
            totals.append(total)
        totals = [spread(jnp.sum(total, axis=1, keepdims=True)) for total in totals]
        potentials = [
            log_mass[rows_of(table.order(place)), :] - (peak + jnp.log2(total))
            for place, peak, total in zip(places, peaks, totals)
        ]
        for place, potential in zip(places, potentials):
            for pair in pairs_of(count):
                tile = scores[place, :, span(pair)] + wide(potential, pair)
                top = jnp.max(tile, axis=0, keepdims=True)
                row = top + jnp.log2(jnp.sum(jnp.exp2(tile - top), axis=0, keepdims=True))
                put_rows(rows, place, pair, row)

    table.by_groups(body, 1)

    def join(step, carry):
        for k in range(JOINED):
            block = step * JOINED + k
            picked = jnp.where(slot_ref[...] == block, rows[...], FLOOR)
            top = jnp.max(picked, axis=0, keepdims=True)
            total = jnp.sum(jnp.exp2(picked - top), axis=0, keepdims=True)
            lse[pl.ds(block, 1), :] = top + jnp.log2(total)
        return carry

    lax.fori_loop(0, ref_blocks // JOINED, join, 0)


def second_kernel(table, scores, pot, log_mass, onehot, weights, peaks, sums, rows):
    run_blocks = weights.shape[0]
    table = Table(table, run_blocks)
    rows[...] = jnp.zeros_like(rows)

    def body(count, places):
        tops = []
        for place in places:
            peak = None
            for pair in pairs_of(count):
                tile = scores[place, :, span(pair)] + pair_row(pot, table, place, pair)
                top = halves(jnp.maximum, tile)
                peak = top if peak is None else jnp.maximum(peak, top)
            tops.append(peak)
        tops = [spread(jnp.max(peak, axis=1, keepdims=True)) for peak in tops]
        totals = []
        for place, peak in zip(places, tops):
            peaks[rows_of(place), :] = peak
            total = None
            for pair in pairs_of(count):
                tile = scores[place, :, span(pair)] + pair_row(pot, table, place, pair)
                weight = jnp.exp2(tile - wide(peak, pair))
                weights[place, :, span(pair)] = weight
                part = halves(jnp.add, weight)
                total = part if total is None else total + part
            totals.append(total)
        totals = [spread(jnp.sum(total, axis=1, keepdims=True)) for total in totals]
        factors = [
            jnp.exp2(log_mass[rows_of(table.order(place)), :] - jnp.log2(total))
            for place, total in zip(places, totals)
        ]
        for place, factor in zip(places, factors):
            for pair in pairs_of(count):
                weight = weights[place, :, span(pair)] * wide(factor, pair)
                put_rows(rows, place, pair, jnp.sum(weight, axis=0, keepdims=True))

    table.by_groups(body, 2)
    sums[...] = jnp.dot(
        onehot[...],
        rows[...],
        precision=lax.Precision.HIGHEST,
        preferred_element_type=jnp.float32,
    )


def third_kernel(table, weights, peaks, gain, log_mass, onehot, out, sums, rows):
    run_blocks = weights.shape[0]
    table = Table(table, run_blocks)
    rows[...] = jnp.zeros_like(rows)
    diagonal = lax.broadcasted_iota(jnp.int32, (BLK, BLK), 0) == lax.broadcasted_iota(
        jnp.int32, (BLK, BLK), 1
    )

    def body(count, places):
        totals = []
        for place in places:
            total = None
            for pair in pairs_of(count):
                weight = weights[place, :, span(pair)] * pair_row(gain, table, place, pair)
                part = halves(jnp.add, weight)
                total = part if total is None else total + part
            totals.append(total)
        totals = [spread(jnp.sum(total, axis=1, keepdims=True)) for total in totals]
        factors = []
        for place, total in zip(places, totals):
            block = table.order(place)
            log_factor = log_mass[rows_of(block), :] - jnp.log2(total)
            factors.append(jnp.exp2(log_factor))
            potential = (log_factor - peaks[rows_of(place), :]) * (0.5 / LOG2E)
            out[pl.ds(block, 1), :] = jnp.sum(
                jnp.where(diagonal, potential, 0.0), axis=0, keepdims=True
            )
        for place, factor in zip(places, factors):
            for pair in pairs_of(count):
                weight = weights[place, :, span(pair)] * wide(factor, pair)
                put_rows(rows, place, pair, jnp.sum(weight, axis=0, keepdims=True))

    table.by_groups(body, 2)
    total = jnp.dot(
        onehot[...],
        rows[...],
        precision=lax.Precision.HIGHEST,
        preferred_element_type=jnp.float32,
    )
    for group in range(sums.shape[0]):
        sums[group] = total


def in_hbm(value):
    return pltpu.with_memory_space_constraint(value, pltpu.HBM)


def in_vmem(value):
    return pltpu.with_memory_space_constraint(value, pltpu.VMEM)


def call(kernel, ins, outs, scratch, aliases={}):
    return pl.pallas_call(
        kernel,
        in_specs=ins,
        out_specs=[vmem] * len(outs),
        out_shape=outs,
        scratch_shapes=scratch,
        input_output_aliases=aliases,
        compiler_params=pltpu.CompilerParams(vmem_limit_bytes=VMEM_LIMIT),
    )


def by_twos(join, parts):
    while len(parts) > 1:
        parts = [join(*parts[k : k + 2]) for k in range(0, len(parts), 2)]
    return parts[0]


def log_sum(parts):
    top = by_twos(jnp.maximum, parts)
    return top + jnp.log2(by_twos(jnp.add, [jnp.exp2(part - top) for part in parts]))


def plain_sum(parts):
    return by_twos(jnp.add, parts)


class Links:
    def __init__(self, groups, width):
        self.width = width
        self.groups = groups
        self.devices = groups * width

    def swap(self, value, mask):
        pairs = [(k, k ^ mask) for k in range(self.devices)]
        return lax.ppermute(value, ("grp", "nar"), pairs)

    def reduce_all(self, value, join):
        masks, bit = [[1]], 2
        while bit < self.devices:
            wide = 4 * bit <= self.devices
            masks.append([bit, 2 * bit, 3 * bit] if wide else [bit])
            bit *= 4 if wide else 2
        for stage in masks:
            value = join([value] + [self.swap(value, mask) for mask in stage])
        return value

    def reduce_own(self, copies, join):
        own = copies.shape[1] // self.width
        sent = copies.reshape(self.devices, own, BLK)
        return join(list(lax.all_to_all(sent, ("grp", "nar"), 0, 0, tiled=True)))

    def gather(self, value):
        held = {0: value}
        mask = self.width // 2
        while mask:
            held.update({key ^ mask: self.swap(part, mask) for key, part in list(held.items())})
            mask //= 2
        return [held[key] for key in range(self.width)]

    def gather_pieces(self, value):
        me = lax.axis_index("nar")
        side = lax.axis_index("grp") % 2
        rows = value.shape[0]
        cut = rows // 4 // BLK * BLK
        parted = self.width > 2 and self.groups % 2 == 0 and cut > 0
        mask = self.width // 2
        held = {0: [(value, 0)]}
        while mask:
            for key, pieces in list(held.items()):
                if parted and key == 0 and mask == self.width // 2:
                    start = side * (rows - cut)
                    near = self.swap(lax.dynamic_slice_in_dim(value, start, cut, 0), mask)
                    middle = self.swap(value[cut : rows - cut], mask)
                    far = self.swap(near, self.width)
                    got = [(near, start), (far, (1 - side) * (rows - cut)), (middle, cut)]
                else:
                    got = [(self.swap(part, mask), start) for part, start in pieces]
                held[key ^ mask] = got
            mask //= 2
        parts = [part for key in held for part, _ in held[key]]
        starts = [(key ^ me) * rows + start for key in held for _, start in held[key]]
        return parts, jnp.stack([jnp.asarray(start, jnp.int32) for start in starts])

    def arrange(self, parts):
        me = lax.axis_index("nar")
        bit = 1
        parts = list(parts)
        while bit < self.width:
            flip = (me & bit) != 0
            parts = [
                jnp.where(flip, parts[key ^ bit], parts[key]) for key in range(self.width)
            ]
            bit *= 2
        return jnp.concatenate(parts, axis=0)


def shards(run_desc, ref_desc, candidates, live_slots, run_mass, ref_mass, ref_start):
    run_blocks = candidates.shape[0]
    links = Links(lax.axis_size("grp"), lax.axis_size("nar"))
    own_blocks = ref_desc.shape[0] // BLK
    ref_blocks = own_blocks * links.width
    depth = run_desc.shape[1]
    f32 = jnp.float32

    shape = (own_blocks, BLK)
    both = links.gather(jnp.stack([ref_start.reshape(shape), ref_mass.reshape(shape)]))
    pot = links.arrange([part[0] for part in both]) * (2.0 * LOG2E)
    log_ref = jnp.log2(links.arrange([part[1] for part in both]))
    pieces, offsets = links.gather_pieces(ref_desc)
    blocks = jnp.arange(run_blocks, dtype=jnp.int32)
    rank_key = live_slots * run_blocks - blocks
    place = jnp.sum((rank_key[None, :] > rank_key[:, None]).astype(jnp.int32), axis=1)
    moved = place[None, :] == blocks[:, None]
    order = jnp.sum(jnp.where(moved, blocks[None, :], 0), axis=1)
    cand = jnp.sum(jnp.where(moved[:, :, None], candidates[None], 0), axis=1)
    live = jnp.sum(jnp.where(moved, live_slots[None, :], 0), axis=1)
    slots = jnp.arange(TOPC, dtype=jnp.int32)
    eff = jnp.where(slots[None, :] < live[:, None], cand, ref_blocks)
    table = jnp.concatenate([order, live, cand.reshape(-1), eff.reshape(-1), offsets])
    tiles = run_blocks * TOPC
    slot_ref = jnp.broadcast_to(eff.reshape(tiles, 1), (tiles, BLK))
    onehot = (
        eff.reshape(1, tiles) == jnp.arange(ref_blocks, dtype=jnp.int32)[:, None]
    ).astype(f32)

    def padded(table):
        return jnp.concatenate([table, jnp.full((8, BLK), FLOOR, f32)], axis=0)

    rows = pltpu.VMEM((tiles, BLK), f32)
    score_shape = pltpu.VMEM((run_blocks, BLK, TOPC * BLK), f32)
    table_shape = jax.ShapeDtypeStruct((ref_blocks, BLK), f32)
    rep_shape = pltpu.VMEM((run_blocks * BLK, BLK), f32)
    scores, log_mass, lse = call(
        first_kernel,
        [smem] + [pl.BlockSpec(memory_space=pltpu.HBM)] * 3 + [vmem] * (2 + len(pieces) - 1),
        [score_shape, rep_shape, table_shape],
        [
            rows,
            pltpu.VMEM((ref_blocks, depth, BLK), ref_desc.dtype),
            pltpu.VMEM(run_desc.shape, run_desc.dtype),
            pltpu.VMEM((run_blocks, BLK), f32),
            pltpu.VMEM(ref_desc.shape, ref_desc.dtype),
            pltpu.SemaphoreType.DMA((3,)),
        ],
    )(
        table,
        in_hbm(run_desc),
        in_hbm(run_mass.reshape(run_blocks, BLK)),
        in_hbm(pieces[0]),
        padded(pot),
        slot_ref,
        *pieces[1:],
    )

    pot = log_ref - links.reduce_all(lse, log_sum)

    weights, peaks, sums = call(
        second_kernel, [smem] + [vmem] * 4, [score_shape, rep_shape, table_shape], [rows], {1: 0}
    )(table, in_vmem(scores), padded(pot), log_mass, onehot)
    log_gain = log_ref - jnp.log2(links.reduce_all(sums, plain_sum))
    pot = pot + log_gain
    gain = jnp.concatenate([jnp.exp2(log_gain), jnp.zeros((8, BLK), f32)], axis=0)

    run_pot, sums = call(
        third_kernel,
        [smem] + [vmem] * 5,
        [
            jax.ShapeDtypeStruct((run_blocks, BLK), f32),
            jax.ShapeDtypeStruct((links.groups, ref_blocks, BLK), f32),
        ],
        [rows],
    )(table, in_vmem(weights), in_vmem(peaks), gain, log_mass, onehot)
    total = links.reduce_own(sums, plain_sum)
    start = lax.axis_index("nar") * own_blocks

    def mine(table):
        return lax.dynamic_slice_in_dim(table, start, own_blocks, 0)

    own = (mine(log_ref) + mine(pot) - mine(log_gain) - jnp.log2(total)) * (0.5 / LOG2E)
    return run_pot.reshape(-1), own.reshape(-1)


def solution(mesh):
    return jax.shard_map(
        shards,
        mesh=mesh,
        in_specs=(
            P(("grp", "nar"), None),
            P("nar", None),
            P(("grp", "nar"), None),
            P(("grp", "nar")),
            P(("grp", "nar")),
            P("nar"),
            P("nar"),
        ),
        out_specs=(P(("grp", "nar")), P("nar")),
        check_vma=False,
    )
```

```python
import functools
import math

import jax
import jax.numpy as jnp
from jax import lax
from jax.experimental import pallas as pl
from jax.experimental.pallas import tpu as pltpu
from jax.sharding import PartitionSpec as P

BLK = 128
TOPC = 8
JOINED = 8
LOG2E = math.log2(math.e)
FLOOR = -1e30
VMEM_LIMIT = 8 * 1024 * 1024

vmem = pl.BlockSpec(memory_space=pltpu.VMEM)
smem = pl.BlockSpec(memory_space=pltpu.SMEM)


def group_size(run_blocks):
    for size in (4, 2):
        if run_blocks % size == 0:
            return size
    return 1


class Table:
    def __init__(self, ref, run_blocks, ref_blocks):
        self.ref = ref
        self.run_blocks = run_blocks
        self.ref_blocks = ref_blocks

    def order(self, place):
        return self.ref[place]

    def live(self, place):
        return self.ref[self.run_blocks + self.order(place)]

    def cand(self, place, slot):
        return self.ref[(2 + slot) * self.run_blocks + self.order(place)]

    def eff(self, place, slot):
        return jnp.where(slot < self.live(place), self.cand(place, slot), self.ref_blocks)

    def offset(self, index):
        return self.ref[(2 + TOPC) * self.run_blocks + index]

    def by_groups(self, body, grain):
        size = group_size(self.run_blocks)

        def step(group, carry):
            most = self.live(group * size)
            for count in range(grain, TOPC + 1, grain):

                @pl.when((most <= count) & (most > count - grain))
                def _():
                    body(count, [group * size + k for k in range(size)])

            return carry

        lax.fori_loop(0, self.run_blocks // size, step, 0)


def rows_of(block):
    return pl.ds(pl.multiple_of(block * BLK, BLK), BLK)


def side(parts):
    return parts[0] if len(parts) == 1 else jnp.concatenate(parts, axis=1)


def pair_row(values, table, place, pair):
    return side([values[pl.ds(table.eff(place, slot), 1), :] for slot in pair])


def spread(column):
    return jnp.broadcast_to(column, (BLK, BLK))


def wide(tile, pair):
    return side([tile] * len(pair))


def pairs_of(count):
    return [range(first, min(first + 2, count)) for first in range(0, count, 2)]


def span(pair):
    return slice(BLK * pair[0], BLK * (pair[-1] + 1))


def put_rows(rows, block, pair, row):
    for index, slot in enumerate(pair):
        at = block + slot * (rows.shape[0] // TOPC)
        rows[pl.ds(at, 1), :] = row[:, BLK * index : BLK * (index + 1)]


def halves(join, tile):
    return tile if tile.shape[1] == BLK else join(tile[:, :BLK], tile[:, BLK:])


def first_kernel(table, run_hbm, mass_hbm, own_hbm, pot, slot_ref, *rest):
    pieces, (scores, log_mass, lse, rows, ref, run, run_mass, own, arrived) = rest[:-9], rest[-9:]
    run_blocks = scores.shape[0]
    table = Table(table, run_blocks, lse.shape[0])
    copies = [
        pltpu.make_async_copy(mass_hbm, run_mass, arrived.at[0]),
        pltpu.make_async_copy(own_hbm, own, arrived.at[1]),
        pltpu.make_async_copy(run_hbm, run, arrived.at[2]),
    ]
    for copy in copies:
        copy.start()
    own_blocks = own_hbm.shape[0] // BLK
    for index, piece in enumerate(pieces):
        start = table.offset(index + 1) // BLK
        for block in range(piece.shape[0] // BLK):
            ref[start + block] = piece[BLK * block : BLK * (block + 1), :].T
    copies[0].wait()

    def fill(block, carry):
        row = jnp.log2(run_mass[pl.ds(block, 1), :])
        log_mass[rows_of(block), :] = jnp.broadcast_to(row, (BLK, BLK)).T
        return carry

    lax.fori_loop(0, run_blocks, fill, 0, unroll=math.gcd(run_blocks, 8))
    copies[1].wait()
    for block in range(own_blocks):
        ref[table.offset(0) // BLK + block] = own[BLK * block : BLK * (block + 1), :].T
    copies[2].wait()
    ref_blocks = lse.shape[0]
    scale = 2.0 * LOG2E / math.sqrt(run.shape[1])

    def body(count, places):
        peaks = []
        for place in places:
            mine = run[rows_of(table.order(place)), :]
            peak = None
            for pair in pairs_of(count):
                both = jnp.concatenate(
                    [ref[table.cand(place, slot)] for slot in pair], axis=1
                )
                tile = lax.dot_general(
                    mine, both, (((1,), (0,)), ((), ())), preferred_element_type=jnp.float32
                )
                tile = tile * scale
                scores[place, :, span(pair)] = tile
                if len(pair) == 1:
                    scores[place, :, span([count])] = jnp.zeros_like(tile)
                top = halves(jnp.maximum, tile + pair_row(pot, table, place, pair))
                peak = top if peak is None else jnp.maximum(peak, top)
            peaks.append(peak)
        peaks = [spread(jnp.max(peak, axis=1, keepdims=True)) for peak in peaks]
        totals = []
        for place, peak in zip(places, peaks):
            total = None
            for pair in pairs_of(count):
                tile = scores[place, :, span(pair)] + pair_row(pot, table, place, pair)
                part = halves(jnp.add, jnp.exp2(tile - wide(peak, pair)))
                total = part if total is None else total + part
            totals.append(total)
        totals = [spread(jnp.sum(total, axis=1, keepdims=True)) for total in totals]
        potentials = [
            log_mass[rows_of(table.order(place)), :] - (peak + jnp.log2(total))
            for place, peak, total in zip(places, peaks, totals)
        ]
        for place, potential in zip(places, potentials):
            for pair in pairs_of(count):
                tile = scores[place, :, span(pair)] + wide(potential, pair)
                top = jnp.max(tile, axis=0, keepdims=True)
                row = top + jnp.log2(jnp.sum(jnp.exp2(tile - top), axis=0, keepdims=True))
                put_rows(rows, table.order(place), pair, row)

    table.by_groups(body, 1)

    def join(step, carry):
        for k in range(JOINED):
            block = step * JOINED + k
            picked = jnp.where(slot_ref[...] == block, rows[...], FLOOR)
            top = jnp.max(picked, axis=0, keepdims=True)
            total = jnp.sum(jnp.exp2(picked - top), axis=0, keepdims=True)
            lse[pl.ds(block, 1), :] = top + jnp.log2(total)
        return carry

    lax.fori_loop(0, ref_blocks // JOINED, join, 0)


def second_kernel(table, scores, pot, log_mass, onehot, weights, peaks, sums, rows):
    run_blocks = weights.shape[0]
    table = Table(table, run_blocks, pot.shape[0] - 8)
    rows[...] = jnp.zeros_like(rows)

    def body(count, places):
        tops = []
        for place in places:
            peak = None
            for pair in pairs_of(count):
                tile = scores[place, :, span(pair)] + pair_row(pot, table, place, pair)
                top = halves(jnp.maximum, tile)
                peak = top if peak is None else jnp.maximum(peak, top)
            tops.append(peak)
        tops = [spread(jnp.max(peak, axis=1, keepdims=True)) for peak in tops]
        totals = []
        for place, peak in zip(places, tops):
            peaks[rows_of(place), :] = peak
            total = None
            for pair in pairs_of(count):
                tile = scores[place, :, span(pair)] + pair_row(pot, table, place, pair)
                weight = jnp.exp2(tile - wide(peak, pair))
                weights[place, :, span(pair)] = weight
                part = halves(jnp.add, weight)
                total = part if total is None else total + part
            totals.append(total)
        totals = [spread(jnp.sum(total, axis=1, keepdims=True)) for total in totals]
        factors = [
            jnp.exp2(log_mass[rows_of(table.order(place)), :] - jnp.log2(total))
            for place, total in zip(places, totals)
        ]
        for place, factor in zip(places, factors):
            for pair in pairs_of(count):
                weight = weights[place, :, span(pair)] * wide(factor, pair)
                put_rows(rows, table.order(place), pair, jnp.sum(weight, axis=0, keepdims=True))

    table.by_groups(body, 2)
    sums[...] = jnp.dot(
        onehot[...],
        rows[...],
        precision=lax.Precision.HIGHEST,
        preferred_element_type=jnp.float32,
    )


def third_kernel(table, weights, peaks, gain, log_mass, onehot, out, sums, rows):
    run_blocks = weights.shape[0]
    table = Table(table, run_blocks, gain.shape[0] - 8)
    rows[...] = jnp.zeros_like(rows)
    diagonal = lax.broadcasted_iota(jnp.int32, (BLK, BLK), 0) == lax.broadcasted_iota(
        jnp.int32, (BLK, BLK), 1
    )

    def body(count, places):
        totals = []
        for place in places:
            total = None
            for pair in pairs_of(count):
                weight = weights[place, :, span(pair)] * pair_row(gain, table, place, pair)
                part = halves(jnp.add, weight)
                total = part if total is None else total + part
            totals.append(total)
        totals = [spread(jnp.sum(total, axis=1, keepdims=True)) for total in totals]
        factors = []
        for place, total in zip(places, totals):
            block = table.order(place)
            log_factor = log_mass[rows_of(block), :] - jnp.log2(total)
            factors.append(jnp.exp2(log_factor))
            potential = (log_factor - peaks[rows_of(place), :]) * (0.5 / LOG2E)
            out[pl.ds(block, 1), :] = jnp.sum(
                jnp.where(diagonal, potential, 0.0), axis=0, keepdims=True
            )
        for place, factor in zip(places, factors):
            for pair in pairs_of(count):
                weight = weights[place, :, span(pair)] * wide(factor, pair)
                put_rows(rows, table.order(place), pair, jnp.sum(weight, axis=0, keepdims=True))

    table.by_groups(body, 2)
    total = jnp.dot(
        onehot[...],
        rows[...],
        precision=lax.Precision.HIGHEST,
        preferred_element_type=jnp.float32,
    )
    for group in range(sums.shape[0]):
        sums[group] = total


def in_hbm(value):
    return pltpu.with_memory_space_constraint(value, pltpu.HBM)


def in_vmem(value):
    return pltpu.with_memory_space_constraint(value, pltpu.VMEM)


def call(kernel, ins, outs, scratch, aliases={}):
    return pl.pallas_call(
        kernel,
        in_specs=ins,
        out_specs=[vmem] * len(outs),
        out_shape=outs,
        scratch_shapes=scratch,
        input_output_aliases=aliases,
        compiler_params=pltpu.CompilerParams(vmem_limit_bytes=VMEM_LIMIT),
    )


def by_twos(join, parts):
    while len(parts) > 1:
        parts = [join(*parts[k : k + 2]) for k in range(0, len(parts), 2)]
    return parts[0]


def log_sum(parts):
    top = by_twos(jnp.maximum, parts)
    return top + jnp.log2(by_twos(jnp.add, [jnp.exp2(part - top) for part in parts]))


def plain_sum(parts):
    return by_twos(jnp.add, parts)


class Links:
    def __init__(self, groups, width):
        self.width = width
        self.groups = groups
        self.devices = groups * width

    def swap(self, value, mask):
        pairs = [(k, k ^ mask) for k in range(self.devices)]
        return lax.ppermute(value, ("grp", "nar"), pairs)

    def reduce_all(self, value, join):
        masks, bit = [[1]], 2
        while bit < self.devices:
            wide = 4 * bit <= self.devices
            stage = [bit, 2 * bit, 3 * bit] if wide else [bit]
            masks.append([mask ^ 1 for mask in stage])
            bit *= 4 if wide else 2
        for stage in masks:
            value = join([value] + [self.swap(value, mask) for mask in stage])
        return value

    def reduce_own(self, copies, join):
        own = copies.shape[1] // self.width
        sent = copies.reshape(self.devices, own, BLK)
        return join(list(lax.all_to_all(sent, ("grp", "nar"), 0, 0, tiled=True)))

    def masks(self):
        steps, bit = [], self.width // 2
        while bit > 1:
            steps.append(bit ^ 1)
            bit //= 2
        return steps + [1] * (self.width > 1)

    def gather(self, value):
        held = {0: value}
        for mask in self.masks():
            held.update({key ^ mask: self.swap(part, mask) for key, part in list(held.items())})
        return [held[key] for key in range(self.width)]

    def gather_pieces(self, value):
        me = lax.axis_index("nar")
        side = lax.axis_index("grp") % 2
        rows = value.shape[0]
        cut = rows // 4 // BLK * BLK
        parted = self.width > 2 and self.groups % 2 == 0 and cut > 0
        held = {0: [(value, 0)]}
        for step, mask in enumerate(self.masks()):
            for key, pieces in list(held.items()):
                if parted and step == 0:
                    start = side * (rows - cut)
                    near = self.swap(lax.dynamic_slice_in_dim(value, start, cut, 0), mask)
                    middle = self.swap(value[cut : rows - cut], mask)
                    far = self.swap(near, self.width)
                    got = [(near, start), (far, (1 - side) * (rows - cut)), (middle, cut)]
                else:
                    got = [(self.swap(part, mask), start) for part, start in pieces]
                held[key ^ mask] = got
        parts = [part for key in held for part, _ in held[key]]
        starts = [(key ^ me) * rows + start for key in held for _, start in held[key]]
        return parts, jnp.stack([jnp.asarray(start, jnp.int32) for start in starts])

    def arrange(self, parts):
        me = lax.axis_index("nar")
        bit = 1
        parts = list(parts)
        while bit < self.width:
            flip = (me & bit) != 0
            parts = [
                jnp.where(flip, parts[key ^ bit], parts[key]) for key in range(self.width)
            ]
            bit *= 2
        return jnp.concatenate(parts, axis=0)


def shards(run_desc, ref_desc, candidates, live_slots, run_mass, ref_mass, ref_start):
    run_blocks = candidates.shape[0]
    links = Links(lax.axis_size("grp"), lax.axis_size("nar"))
    own_blocks = ref_desc.shape[0] // BLK
    ref_blocks = own_blocks * links.width
    depth = run_desc.shape[1]
    f32 = jnp.float32

    shape = (own_blocks, BLK)
    both = links.gather(jnp.stack([ref_start.reshape(shape), ref_mass.reshape(shape)]))
    pot = links.arrange([part[0] for part in both]) * (2.0 * LOG2E)
    log_ref = jnp.log2(links.arrange([part[1] for part in both]))
    pieces, offsets = links.gather_pieces(ref_desc)
    blocks = jnp.arange(run_blocks, dtype=jnp.int32)
    rank_key = live_slots * run_blocks - blocks
    place = jnp.sum((rank_key[None, :] > rank_key[:, None]).astype(jnp.int32), axis=1)
    moved = place[None, :] == blocks[:, None]
    order = jnp.sum(jnp.where(moved, blocks[None, :], 0), axis=1)
    cand = candidates.T
    table = jnp.concatenate([order, live_slots, cand.reshape(-1), offsets])
    slots = jnp.arange(TOPC, dtype=jnp.int32)
    eff = jnp.where(slots[:, None] < live_slots[None, :], cand, ref_blocks)
    tiles = run_blocks * TOPC
    slot_ref = jnp.broadcast_to(eff.reshape(tiles, 1), (tiles, BLK))
    onehot = (
        eff.reshape(1, tiles) == jnp.arange(ref_blocks, dtype=jnp.int32)[:, None]
    ).astype(f32)

    def padded(table):
        return jnp.concatenate([table, jnp.full((8, BLK), FLOOR, f32)], axis=0)

    rows = pltpu.VMEM((tiles, BLK), f32)
    score_shape = pltpu.VMEM((run_blocks, BLK, TOPC * BLK), f32)
    table_shape = jax.ShapeDtypeStruct((ref_blocks, BLK), f32)
    rep_shape = pltpu.VMEM((run_blocks * BLK, BLK), f32)
    scores, log_mass, lse = call(
        first_kernel,
        [smem] + [pl.BlockSpec(memory_space=pltpu.HBM)] * 3 + [vmem] * (2 + len(pieces) - 1),
        [score_shape, rep_shape, table_shape],
        [
            rows,
            pltpu.VMEM((ref_blocks, depth, BLK), ref_desc.dtype),
            pltpu.VMEM(run_desc.shape, run_desc.dtype),
            pltpu.VMEM((run_blocks, BLK), f32),
            pltpu.VMEM(ref_desc.shape, ref_desc.dtype),
            pltpu.SemaphoreType.DMA((3,)),
        ],
    )(
        table,
        in_hbm(run_desc),
        in_hbm(run_mass.reshape(run_blocks, BLK)),
        in_hbm(pieces[0]),
        padded(pot),
        slot_ref,
        *pieces[1:],
    )

    pot = log_ref - links.reduce_all(lse, log_sum)

    weights, peaks, sums = call(
        second_kernel, [smem] + [vmem] * 4, [score_shape, rep_shape, table_shape], [rows], {1: 0}
    )(table, in_vmem(scores), padded(pot), log_mass, onehot)
    log_gain = log_ref - jnp.log2(links.reduce_all(sums, plain_sum))
    pot = pot + log_gain
    gain = jnp.concatenate([jnp.exp2(log_gain), jnp.zeros((8, BLK), f32)], axis=0)

    run_pot, sums = call(
        third_kernel,
        [smem] + [vmem] * 5,
        [
            jax.ShapeDtypeStruct((run_blocks, BLK), f32),
            jax.ShapeDtypeStruct((links.groups, ref_blocks, BLK), f32),
        ],
        [rows],
    )(table, in_vmem(weights), in_vmem(peaks), gain, log_mass, onehot)
    total = links.reduce_own(sums, plain_sum)
    start = lax.axis_index("nar") * own_blocks

    def mine(table):
        return lax.dynamic_slice_in_dim(table, start, own_blocks, 0)

    own = (mine(log_ref) + mine(pot) - mine(log_gain) - jnp.log2(total)) * (0.5 / LOG2E)
    return run_pot.reshape(-1), own.reshape(-1)


def solution(mesh):
    return jax.shard_map(
        shards,
        mesh=mesh,
        in_specs=(
            P(("grp", "nar"), None),
            P("nar", None),
            P(("grp", "nar"), None),
            P(("grp", "nar")),
            P(("grp", "nar")),
            P("nar"),
            P("nar"),
        ),
        out_specs=(P(("grp", "nar")), P("nar")),
        check_vma=False,
    )
```

```python
import functools
import math

import jax
import jax.numpy as jnp
from jax import lax
from jax.experimental import pallas as pl
from jax.experimental.pallas import tpu as pltpu
from jax.sharding import PartitionSpec as P

BLK = 128
TOPC = 8
JOINED = 8
LOG2E = math.log2(math.e)
FLOOR = -1e30
VMEM_LIMIT = 8 * 1024 * 1024

vmem = pl.BlockSpec(memory_space=pltpu.VMEM)
smem = pl.BlockSpec(memory_space=pltpu.SMEM)


def group_size(run_blocks):
    for size in (4, 2):
        if run_blocks % size == 0:
            return size
    return 1


class Table:
    def __init__(self, ref, run_blocks, ref_blocks):
        self.ref = ref
        self.run_blocks = run_blocks
        self.ref_blocks = ref_blocks

    def order(self, place):
        return self.ref[place]

    def live(self, place):
        return self.ref[self.run_blocks + self.order(place)]

    def cand(self, place, slot):
        return self.ref[(2 + slot) * self.run_blocks + self.order(place)]

    def eff(self, place, slot):
        return jnp.where(slot < self.live(place), self.cand(place, slot), self.ref_blocks)

    def offset(self, index):
        return self.ref[(2 + TOPC) * self.run_blocks + index]

    def by_groups(self, body, grain):
        size = group_size(self.run_blocks)

        def step(group, carry):
            most = self.live(group * size)
            for count in range(grain, TOPC + 1, grain):

                @pl.when((most <= count) & (most > count - grain))
                def _():
                    body(count, [group * size + k for k in range(size)])

            return carry

        lax.fori_loop(0, self.run_blocks // size, step, 0)


def rows_of(block):
    return pl.ds(pl.multiple_of(block * BLK, BLK), BLK)


def side(parts):
    return parts[0] if len(parts) == 1 else jnp.concatenate(parts, axis=1)


def pair_row(values, table, place, pair):
    return side([values[pl.ds(table.eff(place, slot), 1), :] for slot in pair])


def spread(column):
    return jnp.broadcast_to(column, (BLK, BLK))


def wide(tile, pair):
    return side([tile] * len(pair))


def pairs_of(count):
    return [range(first, min(first + 2, count)) for first in range(0, count, 2)]


def span(pair):
    return slice(BLK * pair[0], BLK * (pair[-1] + 1))


def put_rows(rows, block, pair, row):
    for index, slot in enumerate(pair):
        at = block + slot * (rows.shape[0] // TOPC)
        rows[pl.ds(at, 1), :] = row[:, BLK * index : BLK * (index + 1)]


def halves(join, tile):
    return tile if tile.shape[1] == BLK else join(tile[:, :BLK], tile[:, BLK:])


def first_kernel(table, run_hbm, mass_hbm, own_hbm, pot, slot_ref, *rest):
    pieces, (scores, log_mass, lse, rows, ref, run, run_mass, own, arrived) = rest[:-9], rest[-9:]
    run_blocks = scores.shape[0]
    table = Table(table, run_blocks, lse.shape[0])
    copies = [
        pltpu.make_async_copy(mass_hbm, run_mass, arrived.at[0]),
        pltpu.make_async_copy(own_hbm, own, arrived.at[1]),
        pltpu.make_async_copy(run_hbm, run, arrived.at[2]),
    ]
    for copy in copies:
        copy.start()
    own_blocks = own_hbm.shape[0] // BLK
    for index, piece in enumerate(pieces):
        start = table.offset(index + 1) // BLK
        for block in range(piece.shape[0] // BLK):
            ref[start + block] = piece[BLK * block : BLK * (block + 1), :].T
    copies[0].wait()

    def fill(block, carry):
        row = jnp.log2(run_mass[pl.ds(block, 1), :])
        log_mass[rows_of(block), :] = jnp.broadcast_to(row, (BLK, BLK)).T
        return carry

    lax.fori_loop(0, run_blocks, fill, 0, unroll=math.gcd(run_blocks, 8))
    copies[1].wait()
    for block in range(own_blocks):
        ref[table.offset(0) // BLK + block] = own[BLK * block : BLK * (block + 1), :].T
    copies[2].wait()
    ref_blocks = lse.shape[0]
    scale = 2.0 * LOG2E / math.sqrt(run.shape[1])

    def body(count, places):
        peaks = []
        for place in places:
            mine = run[rows_of(table.order(place)), :]
            peak = None
            for pair in pairs_of(count):
                both = jnp.concatenate(
                    [ref[table.cand(place, slot)] for slot in pair], axis=1
                )
                tile = lax.dot_general(
                    mine, both, (((1,), (0,)), ((), ())), preferred_element_type=jnp.float32
                )
                tile = tile * scale + pair_row(pot, table, place, pair)
                scores[place, :, span(pair)] = tile
                if len(pair) == 1:
                    scores[place, :, span([count])] = jnp.zeros_like(tile)
                top = halves(jnp.maximum, tile)
                peak = top if peak is None else jnp.maximum(peak, top)
            peaks.append(peak)
        peaks = [spread(jnp.max(peak, axis=1, keepdims=True)) for peak in peaks]
        totals = []
        for place, peak in zip(places, peaks):
            total = None
            for pair in pairs_of(count):
                tile = scores[place, :, span(pair)]
                part = halves(jnp.add, jnp.exp2(tile - wide(peak, pair)))
                total = part if total is None else total + part
            totals.append(total)
        totals = [spread(jnp.sum(total, axis=1, keepdims=True)) for total in totals]
        potentials = [
            log_mass[rows_of(table.order(place)), :] - (peak + jnp.log2(total))
            for place, peak, total in zip(places, peaks, totals)
        ]
        for place, potential in zip(places, potentials):
            for pair in pairs_of(count):
                tile = scores[place, :, span(pair)] + wide(potential, pair)
                top = jnp.max(tile, axis=0, keepdims=True)
                row = top + jnp.log2(jnp.sum(jnp.exp2(tile - top), axis=0, keepdims=True))
                put_rows(rows, table.order(place), pair, row)

    table.by_groups(body, 1)

    def join(step, carry):
        for k in range(JOINED):
            block = step * JOINED + k
            picked = jnp.where(slot_ref[...] == block, rows[...], FLOOR)
            top = jnp.max(picked, axis=0, keepdims=True)
            total = jnp.sum(jnp.exp2(picked - top), axis=0, keepdims=True)
            lse[pl.ds(block, 1), :] = top + jnp.log2(total) - pot[pl.ds(block, 1), :]
        return carry

    lax.fori_loop(0, ref_blocks // JOINED, join, 0)


def second_kernel(table, scores, pot, log_mass, onehot, weights, peaks, sums, rows):
    run_blocks = weights.shape[0]
    table = Table(table, run_blocks, pot.shape[0] - 8)
    rows[...] = jnp.zeros_like(rows)

    def body(count, places):
        tops = []
        for place in places:
            peak = None
            for pair in pairs_of(count):
                tile = scores[place, :, span(pair)] + pair_row(pot, table, place, pair)
                weights[place, :, span(pair)] = tile
                top = halves(jnp.maximum, tile)
                peak = top if peak is None else jnp.maximum(peak, top)
            tops.append(peak)
        tops = [spread(jnp.max(peak, axis=1, keepdims=True)) for peak in tops]
        totals = []
        for place, peak in zip(places, tops):
            peaks[rows_of(place), :] = peak
            total = None
            for pair in pairs_of(count):
                weight = jnp.exp2(weights[place, :, span(pair)] - wide(peak, pair))
                weights[place, :, span(pair)] = weight
                part = halves(jnp.add, weight)
                total = part if total is None else total + part
            totals.append(total)
        totals = [spread(jnp.sum(total, axis=1, keepdims=True)) for total in totals]
        factors = [
            jnp.exp2(log_mass[rows_of(table.order(place)), :] - jnp.log2(total))
            for place, total in zip(places, totals)
        ]
        for place, factor in zip(places, factors):
            for pair in pairs_of(count):
                weight = weights[place, :, span(pair)] * wide(factor, pair)
                put_rows(rows, table.order(place), pair, jnp.sum(weight, axis=0, keepdims=True))

    table.by_groups(body, 2)
    sums[...] = jnp.dot(
        onehot[...],
        rows[...],
        precision=lax.Precision.HIGHEST,
        preferred_element_type=jnp.float32,
    )


def third_kernel(table, weights, peaks, gain, log_mass, onehot, out, sums, rows):
    run_blocks = weights.shape[0]
    table = Table(table, run_blocks, gain.shape[0] - 8)
    rows[...] = jnp.zeros_like(rows)
    diagonal = lax.broadcasted_iota(jnp.int32, (BLK, BLK), 0) == lax.broadcasted_iota(
        jnp.int32, (BLK, BLK), 1
    )

    def body(count, places):
        totals = []
        for place in places:
            total = None
            for pair in pairs_of(count):
                weight = weights[place, :, span(pair)] * pair_row(gain, table, place, pair)
                part = halves(jnp.add, weight)
                total = part if total is None else total + part
            totals.append(total)
        totals = [spread(jnp.sum(total, axis=1, keepdims=True)) for total in totals]
        factors = []
        for place, total in zip(places, totals):
            block = table.order(place)
            log_factor = log_mass[rows_of(block), :] - jnp.log2(total)
            factors.append(jnp.exp2(log_factor))
            potential = (log_factor - peaks[rows_of(place), :]) * (0.5 / LOG2E)
            out[pl.ds(block, 1), :] = jnp.sum(
                jnp.where(diagonal, potential, 0.0), axis=0, keepdims=True
            )
        for place, factor in zip(places, factors):
            for pair in pairs_of(count):
                weight = weights[place, :, span(pair)] * wide(factor, pair)
                put_rows(rows, table.order(place), pair, jnp.sum(weight, axis=0, keepdims=True))

    table.by_groups(body, 2)
    total = jnp.dot(
        onehot[...],
        rows[...],
        precision=lax.Precision.HIGHEST,
        preferred_element_type=jnp.float32,
    )
    for group in range(sums.shape[0]):
        sums[group] = total


def in_hbm(value):
    return pltpu.with_memory_space_constraint(value, pltpu.HBM)


def in_vmem(value):
    return pltpu.with_memory_space_constraint(value, pltpu.VMEM)


def call(kernel, ins, outs, scratch, aliases={}):
    return pl.pallas_call(
        kernel,
        in_specs=ins,
        out_specs=[vmem] * len(outs),
        out_shape=outs,
        scratch_shapes=scratch,
        input_output_aliases=aliases,
        compiler_params=pltpu.CompilerParams(vmem_limit_bytes=VMEM_LIMIT),
    )


def by_twos(join, parts):
    while len(parts) > 1:
        parts = [join(*parts[k : k + 2]) for k in range(0, len(parts), 2)]
    return parts[0]


def log_sum(parts):
    top = by_twos(jnp.maximum, parts)
    return top + jnp.log2(by_twos(jnp.add, [jnp.exp2(part - top) for part in parts]))


def plain_sum(parts):
    return by_twos(jnp.add, parts)


class Links:
    def __init__(self, groups, width):
        self.width = width
        self.groups = groups
        self.devices = groups * width

    def swap(self, value, mask):
        pairs = [(k, k ^ mask) for k in range(self.devices)]
        return lax.ppermute(value, ("grp", "nar"), pairs)

    def reduce_all(self, value, join):
        masks, bit = [[1]], 2
        while bit < self.devices:
            wide = 4 * bit <= self.devices
            stage = [bit, 2 * bit, 3 * bit] if wide else [bit]
            masks.append([mask ^ 1 for mask in stage])
            bit *= 4 if wide else 2
        for stage in masks:
            value = join([value] + [self.swap(value, mask) for mask in stage])
        return value

    def reduce_own(self, copies, join):
        own = copies.shape[1] // self.width
        sent = copies.reshape(self.devices, own, BLK)
        return join(list(lax.all_to_all(sent, ("grp", "nar"), 0, 0, tiled=True)))

    def masks(self):
        steps, bit = [], self.width // 2
        while bit > 1:
            steps.append(bit ^ 1)
            bit //= 2
        return steps + [1] * (self.width > 1)

    def gather(self, value):
        held = {0: value}
        for mask in self.masks():
            held.update({key ^ mask: self.swap(part, mask) for key, part in list(held.items())})
        return [held[key] for key in range(self.width)]

    def gather_pieces(self, value):
        me = lax.axis_index("nar")
        side = lax.axis_index("grp") % 2
        rows = value.shape[0]
        cut = rows // 4 // BLK * BLK
        parted = self.width > 2 and self.groups % 2 == 0 and cut > 0
        held = {0: [(value, 0)]}
        for step, mask in enumerate(self.masks()):
            for key, pieces in list(held.items()):
                if parted and step == 0:
                    start = side * (rows - cut)
                    near = self.swap(lax.dynamic_slice_in_dim(value, start, cut, 0), mask)
                    middle = self.swap(value[cut : rows - cut], mask)
                    far = self.swap(near, self.width)
                    got = [(near, start), (far, (1 - side) * (rows - cut)), (middle, cut)]
                else:
                    got = [(self.swap(part, mask), start) for part, start in pieces]
                held[key ^ mask] = got
        parts = [part for key in held for part, _ in held[key]]
        starts = [(key ^ me) * rows + start for key in held for _, start in held[key]]
        return parts, jnp.stack([jnp.asarray(start, jnp.int32) for start in starts])

    def arrange(self, parts):
        me = lax.axis_index("nar")
        bit = 1
        parts = list(parts)
        while bit < self.width:
            flip = (me & bit) != 0
            parts = [
                jnp.where(flip, parts[key ^ bit], parts[key]) for key in range(self.width)
            ]
            bit *= 2
        return jnp.concatenate(parts, axis=0)


def shards(run_desc, ref_desc, candidates, live_slots, run_mass, ref_mass, ref_start):
    run_blocks = candidates.shape[0]
    links = Links(lax.axis_size("grp"), lax.axis_size("nar"))
    own_blocks = ref_desc.shape[0] // BLK
    ref_blocks = own_blocks * links.width
    depth = run_desc.shape[1]
    f32 = jnp.float32

    shape = (own_blocks, BLK)
    both = links.gather(jnp.stack([ref_start.reshape(shape), ref_mass.reshape(shape)]))
    pot = links.arrange([part[0] for part in both]) * (2.0 * LOG2E)
    log_ref = jnp.log2(links.arrange([part[1] for part in both]))
    pieces, offsets = links.gather_pieces(ref_desc)
    blocks = jnp.arange(run_blocks, dtype=jnp.int32)
    rank_key = live_slots * run_blocks - blocks
    place = jnp.sum((rank_key[None, :] > rank_key[:, None]).astype(jnp.int32), axis=1)
    moved = place[None, :] == blocks[:, None]
    order = jnp.sum(jnp.where(moved, blocks[None, :], 0), axis=1)
    cand = candidates.T
    table = jnp.concatenate([order, live_slots, cand.reshape(-1), offsets])
    slots = jnp.arange(TOPC, dtype=jnp.int32)
    eff = jnp.where(slots[:, None] < live_slots[None, :], cand, ref_blocks)
    tiles = run_blocks * TOPC
    slot_ref = jnp.broadcast_to(eff.reshape(tiles, 1), (tiles, BLK))
    onehot = (
        eff.reshape(1, tiles) == jnp.arange(ref_blocks, dtype=jnp.int32)[:, None]
    ).astype(f32)

    def padded(table):
        return jnp.concatenate([table, jnp.full((8, BLK), FLOOR, f32)], axis=0)

    rows = pltpu.VMEM((tiles, BLK), f32)
    score_shape = pltpu.VMEM((run_blocks, BLK, TOPC * BLK), f32)
    table_shape = jax.ShapeDtypeStruct((ref_blocks, BLK), f32)
    rep_shape = pltpu.VMEM((run_blocks * BLK, BLK), f32)
    scores, log_mass, lse = call(
        first_kernel,
        [smem] + [pl.BlockSpec(memory_space=pltpu.HBM)] * 3 + [vmem] * (2 + len(pieces) - 1),
        [score_shape, rep_shape, table_shape],
        [
            rows,
            pltpu.VMEM((ref_blocks, depth, BLK), ref_desc.dtype),
            pltpu.VMEM(run_desc.shape, run_desc.dtype),
            pltpu.VMEM((run_blocks, BLK), f32),
            pltpu.VMEM(ref_desc.shape, ref_desc.dtype),
            pltpu.SemaphoreType.DMA((3,)),
        ],
    )(
        table,
        in_hbm(run_desc),
        in_hbm(run_mass.reshape(run_blocks, BLK)),
        in_hbm(pieces[0]),
        padded(pot),
        slot_ref,
        *pieces[1:],
    )

    change = log_ref - links.reduce_all(lse, log_sum) - pot

    weights, peaks, sums = call(
        second_kernel, [smem] + [vmem] * 4, [score_shape, rep_shape, table_shape], [rows], {1: 0}
    )(table, in_vmem(scores), padded(change), log_mass, onehot)
    log_gain = log_ref - jnp.log2(links.reduce_all(sums, plain_sum))
    pot = pot + change + log_gain
    gain = jnp.concatenate([jnp.exp2(log_gain), jnp.zeros((8, BLK), f32)], axis=0)

    run_pot, sums = call(
        third_kernel,
        [smem] + [vmem] * 5,
        [
            jax.ShapeDtypeStruct((run_blocks, BLK), f32),
            jax.ShapeDtypeStruct((links.groups, ref_blocks, BLK), f32),
        ],
        [rows],
    )(table, in_vmem(weights), in_vmem(peaks), gain, log_mass, onehot)
    total = links.reduce_own(sums, plain_sum)
    start = lax.axis_index("nar") * own_blocks

    def mine(table):
        return lax.dynamic_slice_in_dim(table, start, own_blocks, 0)

    own = (mine(log_ref) + mine(pot) - mine(log_gain) - jnp.log2(total)) * (0.5 / LOG2E)
    return run_pot.reshape(-1), own.reshape(-1)


def solution(mesh):
    return jax.shard_map(
        shards,
        mesh=mesh,
        in_specs=(
            P(("grp", "nar"), None),
            P("nar", None),
            P(("grp", "nar"), None),
            P(("grp", "nar")),
            P(("grp", "nar")),
            P("nar"),
            P("nar"),
        ),
        out_specs=(P(("grp", "nar")), P("nar")),
        check_vma=False,
    )
```

```python
import functools
import math

import jax
import jax.numpy as jnp
from jax import lax
from jax.experimental import pallas as pl
from jax.experimental.pallas import tpu as pltpu
from jax.sharding import PartitionSpec as P

BLK = 128
TOPC = 8
JOINED = 16
LOG2E = math.log2(math.e)
FLOOR = -1e30
VMEM_LIMIT = 8 * 1024 * 1024

vmem = pl.BlockSpec(memory_space=pltpu.VMEM)
smem = pl.BlockSpec(memory_space=pltpu.SMEM)


def group_size(run_blocks, largest):
    while run_blocks % largest:
        largest //= 2
    return largest


class Table:
    def __init__(self, ref, run_blocks, ref_blocks):
        self.ref = ref
        self.run_blocks = run_blocks
        self.ref_blocks = ref_blocks

    def order(self, place):
        return self.ref[place]

    def live(self, place):
        return self.ref[self.run_blocks + self.order(place)]

    def cand(self, place, slot):
        return self.ref[(2 + slot) * self.run_blocks + self.order(place)]

    def eff(self, place, slot):
        return jnp.where(slot < self.live(place), self.cand(place, slot), self.ref_blocks)

    def offset(self, index):
        return self.ref[(2 + TOPC) * self.run_blocks + index]

    def by_groups(self, body, grain, largest=4):
        size = group_size(self.run_blocks, largest)

        def step(group, carry):
            most = self.live(group * size)
            for count in range(grain, TOPC + 1, grain):

                @pl.when((most <= count) & (most > count - grain))
                def _():
                    body(count, [group * size + k for k in range(size)])

            return carry

        lax.fori_loop(0, self.run_blocks // size, step, 0)


def rows_of(block):
    return pl.ds(pl.multiple_of(block * BLK, BLK), BLK)


def side(parts):
    return parts[0] if len(parts) == 1 else jnp.concatenate(parts, axis=1)


def pair_row(values, table, place, pair):
    return side([values[pl.ds(table.eff(place, slot), 1), :] for slot in pair])


def spread(column):
    return jnp.broadcast_to(column, (BLK, BLK))


def wide(tile, pair):
    return side([tile] * len(pair))


def pairs_of(count):
    return [range(first, min(first + 2, count)) for first in range(0, count, 2)]


def span(pair):
    return slice(BLK * pair[0], BLK * (pair[-1] + 1))


def put_rows(rows, block, pair, row):
    for index, slot in enumerate(pair):
        at = block + slot * (rows.shape[0] // TOPC)
        rows[pl.ds(at, 1), :] = row[:, BLK * index : BLK * (index + 1)]


def halves(join, tile):
    return tile if tile.shape[1] == BLK else join(tile[:, :BLK], tile[:, BLK:])


def first_kernel(table, run_hbm, mass_hbm, own_hbm, pot, slot_ref, *rest):
    pieces, (scores, log_mass, lse, rows, ref, run, run_mass, own, arrived) = rest[:-9], rest[-9:]
    run_blocks = scores.shape[0]
    table = Table(table, run_blocks, lse.shape[0])
    copies = [
        pltpu.make_async_copy(mass_hbm, run_mass, arrived.at[0]),
        pltpu.make_async_copy(own_hbm, own, arrived.at[1]),
        pltpu.make_async_copy(run_hbm, run, arrived.at[2]),
    ]
    for copy in copies:
        copy.start()
    own_blocks = own_hbm.shape[0] // BLK
    for index, piece in enumerate(pieces):
        start = table.offset(index + 1) // BLK
        for block in range(piece.shape[0] // BLK):
            ref[start + block] = piece[BLK * block : BLK * (block + 1), :].T
    copies[0].wait()

    def fill(block, carry):
        row = jnp.log2(run_mass[pl.ds(block, 1), :])
        log_mass[rows_of(block), :] = jnp.broadcast_to(row, (BLK, BLK)).T
        return carry

    lax.fori_loop(0, run_blocks, fill, 0, unroll=math.gcd(run_blocks, 8))
    copies[1].wait()
    for block in range(own_blocks):
        ref[table.offset(0) // BLK + block] = own[BLK * block : BLK * (block + 1), :].T
    copies[2].wait()
    ref_blocks = lse.shape[0]
    scale = 2.0 * LOG2E / math.sqrt(run.shape[1])

    def body(count, places):
        peaks = []
        for place in places:
            mine = run[rows_of(table.order(place)), :]
            peak = None
            for pair in pairs_of(count):
                both = jnp.concatenate(
                    [ref[table.cand(place, slot)] for slot in pair], axis=1
                )
                tile = lax.dot_general(
                    mine, both, (((1,), (0,)), ((), ())), preferred_element_type=jnp.float32
                )
                tile = tile * scale + pair_row(pot, table, place, pair)
                scores[place, :, span(pair)] = tile
                if len(pair) == 1:
                    scores[place, :, span([count])] = jnp.zeros_like(tile)
                top = halves(jnp.maximum, tile)
                peak = top if peak is None else jnp.maximum(peak, top)
            peaks.append(peak)
        peaks = [spread(jnp.max(peak, axis=1, keepdims=True)) for peak in peaks]
        totals = []
        for place, peak in zip(places, peaks):
            total = None
            for pair in pairs_of(count):
                tile = scores[place, :, span(pair)]
                part = halves(jnp.add, jnp.exp2(tile - wide(peak, pair)))
                total = part if total is None else total + part
            totals.append(total)
        totals = [spread(jnp.sum(total, axis=1, keepdims=True)) for total in totals]
        potentials = [
            log_mass[rows_of(table.order(place)), :] - (peak + jnp.log2(total))
            for place, peak, total in zip(places, peaks, totals)
        ]
        for place, potential in zip(places, potentials):
            for pair in pairs_of(count):
                tile = scores[place, :, span(pair)] + wide(potential, pair)
                top = jnp.max(tile, axis=0, keepdims=True)
                row = top + jnp.log2(jnp.sum(jnp.exp2(tile - top), axis=0, keepdims=True))
                put_rows(rows, table.order(place), pair, row)

    table.by_groups(body, 1, 8)

    def join(step, carry):
        for k in range(JOINED):
            block = step * JOINED + k
            picked = jnp.where(slot_ref[...] == block, rows[...], FLOOR)
            top = jnp.max(picked, axis=0, keepdims=True)
            total = jnp.sum(jnp.exp2(picked - top), axis=0, keepdims=True)
            lse[pl.ds(block, 1), :] = top + jnp.log2(total) - pot[pl.ds(block, 1), :]
        return carry

    lax.fori_loop(0, ref_blocks // JOINED, join, 0)


def second_kernel(table, scores, pot, log_mass, onehot, weights, peaks, sums, rows):
    run_blocks = weights.shape[0]
    table = Table(table, run_blocks, pot.shape[0] - 8)
    rows[...] = jnp.zeros_like(rows)

    def body(count, places):
        tops = []
        for place in places:
            peak = None
            for pair in pairs_of(count):
                tile = scores[place, :, span(pair)] + pair_row(pot, table, place, pair)
                weights[place, :, span(pair)] = tile
                top = halves(jnp.maximum, tile)
                peak = top if peak is None else jnp.maximum(peak, top)
            tops.append(peak)
        tops = [spread(jnp.max(peak, axis=1, keepdims=True)) for peak in tops]
        totals = []
        for place, peak in zip(places, tops):
            peaks[rows_of(place), :] = peak
            total = None
            for pair in pairs_of(count):
                weight = jnp.exp2(weights[place, :, span(pair)] - wide(peak, pair))
                weights[place, :, span(pair)] = weight
                part = halves(jnp.add, weight)
                total = part if total is None else total + part
            totals.append(total)
        totals = [spread(jnp.sum(total, axis=1, keepdims=True)) for total in totals]
        factors = [
            jnp.exp2(log_mass[rows_of(table.order(place)), :] - jnp.log2(total))
            for place, total in zip(places, totals)
        ]
        for place, factor in zip(places, factors):
            for pair in pairs_of(count):
                weight = weights[place, :, span(pair)] * wide(factor, pair)
                put_rows(rows, table.order(place), pair, jnp.sum(weight, axis=0, keepdims=True))

    table.by_groups(body, 2)
    sums[...] = jnp.dot(
        onehot[...],
        rows[...],
        precision=lax.Precision.HIGHEST,
        preferred_element_type=jnp.float32,
    )


def third_kernel(table, weights, peaks, gain, log_mass, onehot, out, sums, rows):
    run_blocks = weights.shape[0]
    table = Table(table, run_blocks, gain.shape[0] - 8)
    rows[...] = jnp.zeros_like(rows)
    diagonal = lax.broadcasted_iota(jnp.int32, (BLK, BLK), 0) == lax.broadcasted_iota(
        jnp.int32, (BLK, BLK), 1
    )

    def body(count, places):
        totals = []
        for place in places:
            total = None
            for pair in pairs_of(count):
                weight = weights[place, :, span(pair)] * pair_row(gain, table, place, pair)
                part = halves(jnp.add, weight)
                total = part if total is None else total + part
            totals.append(total)
        totals = [spread(jnp.sum(total, axis=1, keepdims=True)) for total in totals]
        factors = []
        for place, total in zip(places, totals):
            block = table.order(place)
            log_factor = log_mass[rows_of(block), :] - jnp.log2(total)
            factors.append(jnp.exp2(log_factor))
            potential = (log_factor - peaks[rows_of(place), :]) * (0.5 / LOG2E)
            out[pl.ds(block, 1), :] = jnp.sum(
                jnp.where(diagonal, potential, 0.0), axis=0, keepdims=True
            )
        for place, factor in zip(places, factors):
            for pair in pairs_of(count):
                weight = weights[place, :, span(pair)] * wide(factor, pair)
                put_rows(rows, table.order(place), pair, jnp.sum(weight, axis=0, keepdims=True))

    table.by_groups(body, 2)
    total = jnp.dot(
        onehot[...],
        rows[...],
        precision=lax.Precision.HIGHEST,
        preferred_element_type=jnp.float32,
    )
    for group in range(sums.shape[0]):
        sums[group] = total


def in_hbm(value):
    return pltpu.with_memory_space_constraint(value, pltpu.HBM)


def in_vmem(value):
    return pltpu.with_memory_space_constraint(value, pltpu.VMEM)


def call(kernel, ins, outs, scratch, aliases={}):
    return pl.pallas_call(
        kernel,
        in_specs=ins,
        out_specs=[vmem] * len(outs),
        out_shape=outs,
        scratch_shapes=scratch,
        input_output_aliases=aliases,
        compiler_params=pltpu.CompilerParams(vmem_limit_bytes=VMEM_LIMIT),
    )


def by_twos(join, parts):
    while len(parts) > 1:
        parts = [join(*parts[k : k + 2]) for k in range(0, len(parts), 2)]
    return parts[0]


def log_sum(parts):
    top = by_twos(jnp.maximum, parts)
    return top + jnp.log2(by_twos(jnp.add, [jnp.exp2(part - top) for part in parts]))


def plain_sum(parts):
    return by_twos(jnp.add, parts)


class Links:
    def __init__(self, groups, width):
        self.width = width
        self.groups = groups
        self.devices = groups * width

    def swap(self, value, mask):
        pairs = [(k, k ^ mask) for k in range(self.devices)]
        return lax.ppermute(value, ("grp", "nar"), pairs)

    def reduce_all(self, value, join):
        masks, bit = [[1]], 2
        while bit < self.devices:
            wide = 4 * bit <= self.devices
            stage = [bit, 2 * bit, 3 * bit] if wide else [bit]
            masks.append([mask ^ 1 for mask in stage])
            bit *= 4 if wide else 2
        for stage in masks:
            value = join([value] + [self.swap(value, mask) for mask in stage])
        return value

    def reduce_own(self, copies, join):
        own = copies.shape[1] // self.width
        sent = copies.reshape(self.devices, own, BLK)
        return join(list(lax.all_to_all(sent, ("grp", "nar"), 0, 0, tiled=True)))

    def masks(self):
        steps, bit = [], self.width // 2
        while bit > 1:
            steps.append(bit ^ 1)
            bit //= 2
        return steps + [1] * (self.width > 1)

    def gather(self, value):
        held = {0: value}
        for mask in self.masks():
            held.update({key ^ mask: self.swap(part, mask) for key, part in list(held.items())})
        return [held[key] for key in range(self.width)]

    def gather_pieces(self, value):
        me = lax.axis_index("nar")
        side = lax.axis_index("grp") % 2
        rows = value.shape[0]
        cut = rows // 4 // BLK * BLK
        parted = self.width > 2 and self.groups % 2 == 0 and cut > 0
        held = {0: [(value, 0)]}
        for step, mask in enumerate(self.masks()):
            for key, pieces in list(held.items()):
                if parted and step == 0:
                    start = side * (rows - cut)
                    near = self.swap(lax.dynamic_slice_in_dim(value, start, cut, 0), mask)
                    middle = self.swap(value[cut : rows - cut], mask)
                    far = self.swap(near, self.width)
                    got = [(near, start), (far, (1 - side) * (rows - cut)), (middle, cut)]
                else:
                    got = [(self.swap(part, mask), start) for part, start in pieces]
                held[key ^ mask] = got
        parts = [part for key in held for part, _ in held[key]]
        starts = [(key ^ me) * rows + start for key in held for _, start in held[key]]
        return parts, jnp.stack([jnp.asarray(start, jnp.int32) for start in starts])

    def arrange(self, parts):
        me = lax.axis_index("nar")
        bit = 1
        parts = list(parts)
        while bit < self.width:
            flip = (me & bit) != 0
            parts = [
                jnp.where(flip, parts[key ^ bit], parts[key]) for key in range(self.width)
            ]
            bit *= 2
        return jnp.concatenate(parts, axis=0)


def shards(run_desc, ref_desc, candidates, live_slots, run_mass, ref_mass, ref_start):
    run_blocks = candidates.shape[0]
    links = Links(lax.axis_size("grp"), lax.axis_size("nar"))
    own_blocks = ref_desc.shape[0] // BLK
    ref_blocks = own_blocks * links.width
    depth = run_desc.shape[1]
    f32 = jnp.float32

    shape = (own_blocks, BLK)
    both = links.gather(jnp.stack([ref_start.reshape(shape), ref_mass.reshape(shape)]))
    pot = links.arrange([part[0] for part in both]) * (2.0 * LOG2E)
    log_ref = jnp.log2(links.arrange([part[1] for part in both]))
    pieces, offsets = links.gather_pieces(ref_desc)
    blocks = jnp.arange(run_blocks, dtype=jnp.int32)
    rank_key = live_slots * run_blocks - blocks
    place = jnp.sum((rank_key[None, :] > rank_key[:, None]).astype(jnp.int32), axis=1)
    moved = place[None, :] == blocks[:, None]
    order = jnp.sum(jnp.where(moved, blocks[None, :], 0), axis=1)
    cand = candidates.T
    table = jnp.concatenate([order, live_slots, cand.reshape(-1), offsets])
    slots = jnp.arange(TOPC, dtype=jnp.int32)
    eff = jnp.where(slots[:, None] < live_slots[None, :], cand, ref_blocks)
    tiles = run_blocks * TOPC
    slot_ref = jnp.broadcast_to(eff.reshape(tiles, 1), (tiles, BLK))
    onehot = (
        eff.reshape(1, tiles) == jnp.arange(ref_blocks, dtype=jnp.int32)[:, None]
    ).astype(f32)

    def padded(table):
        return jnp.concatenate([table, jnp.full((8, BLK), FLOOR, f32)], axis=0)

    rows = pltpu.VMEM((tiles, BLK), f32)
    score_shape = pltpu.VMEM((run_blocks, BLK, TOPC * BLK), f32)
    table_shape = jax.ShapeDtypeStruct((ref_blocks, BLK), f32)
    rep_shape = pltpu.VMEM((run_blocks * BLK, BLK), f32)
    scores, log_mass, lse = call(
        first_kernel,
        [smem] + [pl.BlockSpec(memory_space=pltpu.HBM)] * 3 + [vmem] * (2 + len(pieces) - 1),
        [score_shape, rep_shape, table_shape],
        [
            rows,
            pltpu.VMEM((ref_blocks, depth, BLK), ref_desc.dtype),
            pltpu.VMEM(run_desc.shape, run_desc.dtype),
            pltpu.VMEM((run_blocks, BLK), f32),
            pltpu.VMEM(ref_desc.shape, ref_desc.dtype),
            pltpu.SemaphoreType.DMA((3,)),
        ],
    )(
        table,
        in_hbm(run_desc),
        in_hbm(run_mass.reshape(run_blocks, BLK)),
        in_hbm(pieces[0]),
        padded(pot),
        slot_ref,
        *pieces[1:],
    )

    change = log_ref - links.reduce_all(lse, log_sum) - pot

    weights, peaks, sums = call(
        second_kernel, [smem] + [vmem] * 4, [score_shape, rep_shape, table_shape], [rows], {1: 0}
    )(table, in_vmem(scores), padded(change), log_mass, onehot)
    log_gain = log_ref - jnp.log2(links.reduce_all(sums, plain_sum))
    pot = pot + change + log_gain
    gain = jnp.concatenate([jnp.exp2(log_gain), jnp.zeros((8, BLK), f32)], axis=0)

    run_pot, sums = call(
        third_kernel,
        [smem] + [vmem] * 5,
        [
            jax.ShapeDtypeStruct((run_blocks, BLK), f32),
            jax.ShapeDtypeStruct((links.groups, ref_blocks, BLK), f32),
        ],
        [rows],
    )(table, in_vmem(weights), in_vmem(peaks), gain, log_mass, onehot)
    total = links.reduce_own(sums, plain_sum)
    start = lax.axis_index("nar") * own_blocks

    def mine(table):
        return lax.dynamic_slice_in_dim(table, start, own_blocks, 0)

    own = (mine(log_ref) + mine(pot) - mine(log_gain) - jnp.log2(total)) * (0.5 / LOG2E)
    return run_pot.reshape(-1), own.reshape(-1)


def solution(mesh):
    return jax.shard_map(
        shards,
        mesh=mesh,
        in_specs=(
            P(("grp", "nar"), None),
            P("nar", None),
            P(("grp", "nar"), None),
            P(("grp", "nar")),
            P(("grp", "nar")),
            P("nar"),
            P("nar"),
        ),
        out_specs=(P(("grp", "nar")), P("nar")),
        check_vma=False,
    )
```

```python
import functools
import math

import jax
import jax.numpy as jnp
from jax import lax
from jax.experimental import pallas as pl
from jax.experimental.pallas import tpu as pltpu
from jax.sharding import PartitionSpec as P

BLK = 128
TOPC = 8
JOINED = 32
LOG2E = math.log2(math.e)
FLOOR = -1e30
VMEM_LIMIT = 8 * 1024 * 1024

vmem = pl.BlockSpec(memory_space=pltpu.VMEM)
smem = pl.BlockSpec(memory_space=pltpu.SMEM)


def group_size(run_blocks, largest):
    while run_blocks % largest:
        largest //= 2
    return largest


class Table:
    def __init__(self, ref, run_blocks, ref_blocks):
        self.ref = ref
        self.run_blocks = run_blocks
        self.ref_blocks = ref_blocks

    def order(self, place):
        return self.ref[place]

    def live(self, place):
        return self.ref[self.run_blocks + self.order(place)]

    def cand(self, place, slot):
        return self.ref[(2 + slot) * self.run_blocks + self.order(place)]

    def eff(self, place, slot):
        return jnp.where(slot < self.live(place), self.cand(place, slot), self.ref_blocks)

    def offset(self, index):
        return self.ref[(2 + TOPC) * self.run_blocks + index]

    def by_groups(self, body, grain, largest=4):
        size = group_size(self.run_blocks, largest)

        def step(group, carry):
            most = self.live(group * size)
            for count in range(grain, TOPC + 1, grain):

                @pl.when((most <= count) & (most > count - grain))
                def _():
                    body(count, [group * size + k for k in range(size)])

            return carry

        lax.fori_loop(0, self.run_blocks // size, step, 0)


def rows_of(block):
    return pl.ds(pl.multiple_of(block * BLK, BLK), BLK)


def side(parts):
    return parts[0] if len(parts) == 1 else jnp.concatenate(parts, axis=1)


def pair_row(values, table, place, pair):
    return side([values[pl.ds(table.eff(place, slot), 1), :] for slot in pair])


def spread(column):
    return jnp.broadcast_to(column, (BLK, BLK))


def wide(tile, pair):
    return side([tile] * len(pair))


def pairs_of(count):
    return [range(first, min(first + 2, count)) for first in range(0, count, 2)]


def span(pair):
    return slice(BLK * pair[0], BLK * (pair[-1] + 1))


def put_rows(rows, block, pair, row):
    for index, slot in enumerate(pair):
        at = block + slot * (rows.shape[0] // TOPC)
        rows[pl.ds(at, 1), :] = row[:, BLK * index : BLK * (index + 1)]


def halves(join, tile):
    return tile if tile.shape[1] == BLK else join(tile[:, :BLK], tile[:, BLK:])


def first_kernel(table, run_hbm, mass_hbm, own_hbm, pot, slot_ref, *rest):
    pieces, (scores, log_mass, lse, rows, ref, run, run_mass, own, arrived) = rest[:-9], rest[-9:]
    run_blocks = scores.shape[0]
    table = Table(table, run_blocks, lse.shape[0])
    copies = [
        pltpu.make_async_copy(mass_hbm, run_mass, arrived.at[0]),
        pltpu.make_async_copy(own_hbm, own, arrived.at[1]),
        pltpu.make_async_copy(run_hbm, run, arrived.at[2]),
    ]
    for copy in copies:
        copy.start()
    own_blocks = own_hbm.shape[0] // BLK
    for index, piece in enumerate(pieces):
        start = table.offset(index + 1) // BLK
        for block in range(piece.shape[0] // BLK):
            ref[start + block] = piece[BLK * block : BLK * (block + 1), :].T
    copies[0].wait()

    def fill(block, carry):
        row = jnp.log2(run_mass[pl.ds(block, 1), :])
        log_mass[rows_of(block), :] = jnp.broadcast_to(row, (BLK, BLK)).T
        return carry

    lax.fori_loop(0, run_blocks, fill, 0, unroll=math.gcd(run_blocks, 8))
    copies[1].wait()
    for block in range(own_blocks):
        ref[table.offset(0) // BLK + block] = own[BLK * block : BLK * (block + 1), :].T
    copies[2].wait()
    ref_blocks = lse.shape[0]
    scale = 2.0 * LOG2E / math.sqrt(run.shape[1])

    def body(count, places):
        peaks = []
        for place in places:
            mine = run[rows_of(table.order(place)), :]
            peak = None
            for pair in pairs_of(count):
                both = jnp.concatenate(
                    [ref[table.cand(place, slot)] for slot in pair], axis=1
                )
                tile = lax.dot_general(
                    mine, both, (((1,), (0,)), ((), ())), preferred_element_type=jnp.float32
                )
                tile = tile * scale + pair_row(pot, table, place, pair)
                scores[place, :, span(pair)] = tile
                if len(pair) == 1:
                    scores[place, :, span([count])] = jnp.zeros_like(tile)
                top = halves(jnp.maximum, tile)
                peak = top if peak is None else jnp.maximum(peak, top)
            peaks.append(peak)
        peaks = [spread(jnp.max(peak, axis=1, keepdims=True)) for peak in peaks]
        totals = []
        for place, peak in zip(places, peaks):
            total = None
            for pair in pairs_of(count):
                tile = scores[place, :, span(pair)]
                part = halves(jnp.add, jnp.exp2(tile - wide(peak, pair)))
                total = part if total is None else total + part
            totals.append(total)
        totals = [spread(jnp.sum(total, axis=1, keepdims=True)) for total in totals]
        potentials = [
            log_mass[rows_of(table.order(place)), :] - (peak + jnp.log2(total))
            for place, peak, total in zip(places, peaks, totals)
        ]
        for place, potential in zip(places, potentials):
            for pair in pairs_of(count):
                tile = scores[place, :, span(pair)] + wide(potential, pair)
                top = jnp.max(tile, axis=0, keepdims=True)
                row = top + jnp.log2(jnp.sum(jnp.exp2(tile - top), axis=0, keepdims=True))
                put_rows(rows, table.order(place), pair, row)

    table.by_groups(body, 1, 8)

    def join(step, carry):
        for k in range(JOINED):
            block = step * JOINED + k
            picked = jnp.where(slot_ref[...] == block, rows[...], FLOOR)
            top = jnp.max(picked, axis=0, keepdims=True)
            total = jnp.sum(jnp.exp2(picked - top), axis=0, keepdims=True)
            lse[pl.ds(block, 1), :] = top + jnp.log2(total) - pot[pl.ds(block, 1), :]
        return carry

    lax.fori_loop(0, ref_blocks // JOINED, join, 0)


def second_kernel(table, scores, pot, log_mass, onehot, weights, peaks, sums, rows):
    run_blocks = weights.shape[0]
    table = Table(table, run_blocks, pot.shape[0] - 8)
    rows[...] = jnp.zeros_like(rows)

    def body(count, places):
        tops = []
        for place in places:
            peak = None
            for pair in pairs_of(count):
                tile = scores[place, :, span(pair)] + pair_row(pot, table, place, pair)
                weights[place, :, span(pair)] = tile
                top = halves(jnp.maximum, tile)
                peak = top if peak is None else jnp.maximum(peak, top)
            tops.append(peak)
        tops = [spread(jnp.max(peak, axis=1, keepdims=True)) for peak in tops]
        totals = []
        for place, peak in zip(places, tops):
            peaks[rows_of(place), :] = peak
            total = None
            for pair in pairs_of(count):
                weight = jnp.exp2(weights[place, :, span(pair)] - wide(peak, pair))
                weights[place, :, span(pair)] = weight
                part = halves(jnp.add, weight)
                total = part if total is None else total + part
            totals.append(total)
        totals = [spread(jnp.sum(total, axis=1, keepdims=True)) for total in totals]
        factors = [
            jnp.exp2(log_mass[rows_of(table.order(place)), :] - jnp.log2(total))
            for place, total in zip(places, totals)
        ]
        for place, factor in zip(places, factors):
            for pair in pairs_of(count):
                weight = weights[place, :, span(pair)] * wide(factor, pair)
                put_rows(rows, table.order(place), pair, jnp.sum(weight, axis=0, keepdims=True))

    table.by_groups(body, 2)
    sums[...] = jnp.dot(
        onehot[...],
        rows[...],
        precision=lax.Precision.HIGHEST,
        preferred_element_type=jnp.float32,
    )


def third_kernel(table, weights, peaks, gain, log_mass, onehot, out, sums, rows):
    run_blocks = weights.shape[0]
    table = Table(table, run_blocks, gain.shape[0] - 8)
    rows[...] = jnp.zeros_like(rows)
    diagonal = lax.broadcasted_iota(jnp.int32, (BLK, BLK), 0) == lax.broadcasted_iota(
        jnp.int32, (BLK, BLK), 1
    )

    def body(count, places):
        totals = []
        for place in places:
            total = None
            for pair in pairs_of(count):
                weight = weights[place, :, span(pair)] * pair_row(gain, table, place, pair)
                part = halves(jnp.add, weight)
                total = part if total is None else total + part
            totals.append(total)
        totals = [spread(jnp.sum(total, axis=1, keepdims=True)) for total in totals]
        factors = []
        for place, total in zip(places, totals):
            block = table.order(place)
            log_factor = log_mass[rows_of(block), :] - jnp.log2(total)
            factors.append(jnp.exp2(log_factor))
            potential = (log_factor - peaks[rows_of(place), :]) * (0.5 / LOG2E)
            out[pl.ds(block, 1), :] = jnp.sum(
                jnp.where(diagonal, potential, 0.0), axis=0, keepdims=True
            )
        for place, factor in zip(places, factors):
            for pair in pairs_of(count):
                weight = weights[place, :, span(pair)] * wide(factor, pair)
                put_rows(rows, table.order(place), pair, jnp.sum(weight, axis=0, keepdims=True))

    table.by_groups(body, 2)
    total = jnp.dot(
        onehot[...],
        rows[...],
        precision=lax.Precision.HIGHEST,
        preferred_element_type=jnp.float32,
    )
    for group in range(sums.shape[0]):
        sums[group] = total


def in_hbm(value):
    return pltpu.with_memory_space_constraint(value, pltpu.HBM)


def in_vmem(value):
    return pltpu.with_memory_space_constraint(value, pltpu.VMEM)


def call(kernel, ins, outs, scratch, aliases={}):
    return pl.pallas_call(
        kernel,
        in_specs=ins,
        out_specs=[vmem] * len(outs),
        out_shape=outs,
        scratch_shapes=scratch,
        input_output_aliases=aliases,
        compiler_params=pltpu.CompilerParams(vmem_limit_bytes=VMEM_LIMIT),
    )


def by_twos(join, parts):
    while len(parts) > 1:
        parts = [join(*parts[k : k + 2]) for k in range(0, len(parts), 2)]
    return parts[0]


def log_sum(parts):
    top = by_twos(jnp.maximum, parts)
    return top + jnp.log2(by_twos(jnp.add, [jnp.exp2(part - top) for part in parts]))


def plain_sum(parts):
    return by_twos(jnp.add, parts)


class Links:
    def __init__(self, groups, width):
        self.width = width
        self.groups = groups
        self.devices = groups * width

    def swap(self, value, mask):
        pairs = [(k, k ^ mask) for k in range(self.devices)]
        return lax.ppermute(value, ("grp", "nar"), pairs)

    def reduce_all(self, value, join):
        masks, bit = [[1]], 2
        while bit < self.devices:
            wide = 4 * bit <= self.devices
            stage = [bit, 2 * bit, 3 * bit] if wide else [bit]
            masks.append([mask ^ 1 for mask in stage])
            bit *= 4 if wide else 2
        for stage in masks:
            value = join([value] + [self.swap(value, mask) for mask in stage])
        return value

    def reduce_own(self, copies, join):
        own = copies.shape[1] // self.width
        sent = copies.reshape(self.devices, own, BLK)
        return join(list(lax.all_to_all(sent, ("grp", "nar"), 0, 0, tiled=True)))

    def masks(self):
        steps, bit = [], self.width // 2
        while bit > 1:
            steps.append(bit ^ 1)
            bit //= 2
        return steps + [1] * (self.width > 1)

    def gather(self, value):
        held = {0: value}
        for mask in self.masks():
            held.update({key ^ mask: self.swap(part, mask) for key, part in list(held.items())})
        return [held[key] for key in range(self.width)]

    def gather_pieces(self, value):
        me = lax.axis_index("nar")
        side = lax.axis_index("grp") % 2
        rows = value.shape[0]
        cut = rows // 4 // BLK * BLK
        parted = self.width > 2 and self.groups % 2 == 0 and cut > 0
        held = {0: [(value, 0)]}
        for step, mask in enumerate(self.masks()):
            for key, pieces in list(held.items()):
                if parted and step == 0:
                    start = side * (rows - cut)
                    near = self.swap(lax.dynamic_slice_in_dim(value, start, cut, 0), mask)
                    middle = self.swap(value[cut : rows - cut], mask)
                    far = self.swap(near, self.width)
                    got = [(near, start), (far, (1 - side) * (rows - cut)), (middle, cut)]
                else:
                    got = [(self.swap(part, mask), start) for part, start in pieces]
                held[key ^ mask] = got
        parts = [part for key in held for part, _ in held[key]]
        starts = [(key ^ me) * rows + start for key in held for _, start in held[key]]
        return parts, jnp.stack([jnp.asarray(start, jnp.int32) for start in starts])

    def arrange(self, parts):
        me = lax.axis_index("nar")
        bit = 1
        parts = list(parts)
        while bit < self.width:
            flip = (me & bit) != 0
            parts = [
                jnp.where(flip, parts[key ^ bit], parts[key]) for key in range(self.width)
            ]
            bit *= 2
        return jnp.concatenate(parts, axis=0)


def shards(run_desc, ref_desc, candidates, live_slots, run_mass, ref_mass, ref_start):
    run_blocks = candidates.shape[0]
    links = Links(lax.axis_size("grp"), lax.axis_size("nar"))
    own_blocks = ref_desc.shape[0] // BLK
    ref_blocks = own_blocks * links.width
    depth = run_desc.shape[1]
    f32 = jnp.float32

    shape = (own_blocks, BLK)
    both = links.gather(jnp.stack([ref_start.reshape(shape), ref_mass.reshape(shape)]))
    pot = links.arrange([part[0] for part in both]) * (2.0 * LOG2E)
    log_ref = jnp.log2(links.arrange([part[1] for part in both]))
    pieces, offsets = links.gather_pieces(ref_desc)
    blocks = jnp.arange(run_blocks, dtype=jnp.int32)
    rank_key = live_slots * run_blocks - blocks
    place = jnp.sum((rank_key[None, :] > rank_key[:, None]).astype(jnp.int32), axis=1)
    moved = place[None, :] == blocks[:, None]
    order = jnp.sum(jnp.where(moved, blocks[None, :], 0), axis=1)
    cand = candidates.T
    table = jnp.concatenate([order, live_slots, cand.reshape(-1), offsets])
    slots = jnp.arange(TOPC, dtype=jnp.int32)
    eff = jnp.where(slots[:, None] < live_slots[None, :], cand, ref_blocks)
    tiles = run_blocks * TOPC
    slot_ref = jnp.broadcast_to(eff.reshape(tiles, 1), (tiles, BLK))
    onehot = (
        eff.reshape(1, tiles) == jnp.arange(ref_blocks, dtype=jnp.int32)[:, None]
    ).astype(f32)

    def padded(table):
        return jnp.concatenate([table, jnp.full((8, BLK), FLOOR, f32)], axis=0)

    rows = pltpu.VMEM((tiles, BLK), f32)
    score_shape = pltpu.VMEM((run_blocks, BLK, TOPC * BLK), f32)
    table_shape = jax.ShapeDtypeStruct((ref_blocks, BLK), f32)
    rep_shape = pltpu.VMEM((run_blocks * BLK, BLK), f32)
    scores, log_mass, lse = call(
        first_kernel,
        [smem] + [pl.BlockSpec(memory_space=pltpu.HBM)] * 3 + [vmem] * (2 + len(pieces) - 1),
        [score_shape, rep_shape, table_shape],
        [
            rows,
            pltpu.VMEM((ref_blocks, depth, BLK), ref_desc.dtype),
            pltpu.VMEM(run_desc.shape, run_desc.dtype),
            pltpu.VMEM((run_blocks, BLK), f32),
            pltpu.VMEM(ref_desc.shape, ref_desc.dtype),
            pltpu.SemaphoreType.DMA((3,)),
        ],
    )(
        table,
        in_hbm(run_desc),
        in_hbm(run_mass.reshape(run_blocks, BLK)),
        in_hbm(pieces[0]),
        padded(pot),
        slot_ref,
        *pieces[1:],
    )

    change = log_ref - links.reduce_all(lse, log_sum) - pot

    weights, peaks, sums = call(
        second_kernel, [smem] + [vmem] * 4, [score_shape, rep_shape, table_shape], [rows], {1: 0}
    )(table, in_vmem(scores), padded(change), log_mass, onehot)
    log_gain = log_ref - jnp.log2(links.reduce_all(sums, plain_sum))
    pot = pot + change + log_gain
    gain = jnp.concatenate([jnp.exp2(log_gain), jnp.zeros((8, BLK), f32)], axis=0)

    run_pot, sums = call(
        third_kernel,
        [smem] + [vmem] * 5,
        [
            jax.ShapeDtypeStruct((run_blocks, BLK), f32),
            jax.ShapeDtypeStruct((links.groups, ref_blocks, BLK), f32),
        ],
        [rows],
    )(table, in_vmem(weights), in_vmem(peaks), gain, log_mass, onehot)
    total = links.reduce_own(sums, plain_sum)
    start = lax.axis_index("nar") * own_blocks

    def mine(table):
        return lax.dynamic_slice_in_dim(table, start, own_blocks, 0)

    own = (mine(log_ref) + mine(pot) - mine(log_gain) - jnp.log2(total)) * (0.5 / LOG2E)
    return run_pot.reshape(-1), own.reshape(-1)


def solution(mesh):
    return jax.shard_map(
        shards,
        mesh=mesh,
        in_specs=(
            P(("grp", "nar"), None),
            P("nar", None),
            P(("grp", "nar"), None),
            P(("grp", "nar")),
            P(("grp", "nar")),
            P("nar"),
            P("nar"),
        ),
        out_specs=(P(("grp", "nar")), P("nar")),
        check_vma=False,
    )
```
